32 devices in a mesh: dom: 8 (over z, y), feat: 4 (over x, core).
Axes of the slice: x: 2, y: 2, z: 4, core: 2. Of those that a mesh axis runs over, the one named last changes fastest.
Arguments:
- features: bfloat16 [128, 8192], P('feat', 'dom'), may hold values from -6 to 6
- tile_mask: int32 [192, 6, 128, 128], P('dom'), may hold values 0 or 1
- tile_cols: int32 [192, 6], P('dom'), may hold values from 0 to 23, as said below
- replicas: int32 [3, 16384], P(None, 'dom'), may hold values from 0 to 1023, as said below
- degree: int32 [8192], P('dom'), may hold values from 12 to 47
- self_one: bfloat16 [128, 256], replicated, may hold values from -0.5 to 0.5
- neigh_one: bfloat16 [128, 256], replicated, may hold values from -2 to 2
- self_two: bfloat16 [256, 256], replicated, may hold values from -0.375 to 0.375
- neigh_two: bfloat16 [256, 256], replicated, may hold values from -1.5 to 1.5
Outputs:
- embed: bfloat16 [256, 8192], P('feat', 'dom')
The draws below stay inside these ranges and needn't reach their ends.
Inputs may be any that keep to these rules, and one draw needn't show every extreme that they name: replicas[0] never names the mirror's own partition; a partition's mirrors with one master partition have distinct slots 0 to at most 511 and distinct master rows; in every draw some master partition receives exactly 512 mirrors from every other partition. `tile_cols`: the 6 column blocks of one row of blocks are distinct.
All inputs are finite; a program needn't handle non-finite values. No bound on the sum of `tile_mask` on one device may be relied on, other than what follows from the above.
Results may differ from the reference program's by a relative error of at most 0.0027.
The reference program's roundings to bfloat16 on the way count: a program that leaves them out, or rounds other values in their place, can miss the bound.
Values may be sent and summed in bfloat16 or wider, within the bound.
No kernel may reach another device: no remote copies, remote signals or barrier semaphores. Data moves between devices by JAX's collectives and lax.ppermute only.
A program may use at most 64 MiB of HBM per device.

```python
import jax
import jax.numpy as jnp
from jax import lax

FIN = 128
HID = 256
MAST = 1024
TILE = 128
K = 6
MIRROR_VERTICES = 2048
ROWS = 3072
TILES = 24
EDGE_PARTITIONS = 8
CAP = 512
NM = 8192


def draw_tile_cols(key, part):
    keys = jax.random.split(jax.random.fold_in(key, 11), EDGE_PARTITIONS * TILES)
    chosen = jax.vmap(lambda one_key: jax.random.permutation(one_key, TILES)[:K])(keys)
    return chosen.astype(jnp.int32)


def draw_replicas(key, part):
    partition_count = EDGE_PARTITIONS
    hot_dest = jax.random.randint(jax.random.fold_in(key, 1), (), 0, partition_count)
    offset = jax.random.randint(jax.random.fold_in(key, 2), (partition_count, 1), 0, partition_count)
    row_shift = jax.random.randint(jax.random.fold_in(key, 3), (partition_count, partition_count), 0, MAST)
    source = jnp.arange(partition_count)[:, None]
    mirror_row_index = jnp.arange(MIRROR_VERTICES)[None, :]
    lower_end = jnp.minimum(source, hot_dest)
    upper_end = jnp.maximum(source, hot_dest)
    remaining = mirror_row_index - CAP
    chosen = (remaining + offset) % (partition_count - 2)
    chosen = chosen + (chosen >= lower_end)
    chosen = chosen + (chosen >= upper_end)
    dest_cold = jnp.where(mirror_row_index < CAP, hot_dest, chosen)
    slot_cold = jnp.where(mirror_row_index < CAP, mirror_row_index, remaining // (partition_count - 2))
    chosen_hot = (mirror_row_index + offset) % (partition_count - 1)
    chosen_hot = chosen_hot + (chosen_hot >= source)
    slot_hot = mirror_row_index // (partition_count - 1)
    is_hot = source == hot_dest
    destination = jnp.where(is_hot, chosen_hot, dest_cold)
    slot_rank = jnp.where(is_hot, slot_hot, slot_cold)
    shift_here = row_shift[jnp.broadcast_to(source, destination.shape), destination]
    master_row = (slot_rank * 37 + shift_here) % MAST
    stacked_rows = jnp.stack([destination, slot_rank, master_row])
    return stacked_rows.reshape(3, partition_count * MIRROR_VERTICES).astype(jnp.int32)


def plant(drawn, rng, smallest, top_value):
    extent = drawn.shape
    spot = [jax.random.randint(jax.random.fold_in(rng, axis), (), 0, extent[axis]) for axis in range(len(extent))]
    drawn = drawn.at[tuple(spot)].set(smallest)
    longest = extent.index(max(extent))
    spot[longest] = (spot[longest] + 1) % extent[longest]
    return drawn.at[tuple(spot)].set(top_value)


def steps_of(own_key, extent, shards, smallest, top_value):
    def one(axis_at, shards_of):
        draws = jax.random.uniform(jax.random.fold_in(jax.random.fold_in(own_key, 6), axis_at), (shards_of,), jnp.float32, smallest / len(shards), top_value / len(shards))
        return jnp.repeat(jnp.exp(draws), extent[axis_at] // shards_of).reshape((-1,) + (1,) * (len(extent) - axis_at - 1))

    gain = one(*shards[0])
    for cut in shards[1:]:
        gain = gain * one(*cut)
    return gain


def centred(key, shape, width, most, cuts=(), held_as=jnp.bfloat16):
    gain = steps_of(key, shape, cuts, -0.22, 0.18) if cuts else 1.0
    entries = jax.random.normal(key, shape, jnp.float32) * width * gain
    return jnp.minimum(jnp.maximum(entries, -most), most).astype(held_as)


def setup_inputs(seed: int = 0) -> dict:
    key_of = jax.random.split(jax.random.key(seed), 10)
    features = centred(key_of[0], (FIN, NM), 1.0, 6.0, ((0, 4), (1, 8)))
    tile_mask = plant((jax.random.randint(key_of[1], (EDGE_PARTITIONS * TILES, K, TILE, TILE), 0, K * TILE // 24) < 1).astype(jnp.int32), jax.random.fold_in(key_of[1], 1), 0, 1)
    tile_cols = draw_tile_cols(jax.random.fold_in(key_of[9], 71), 0)
    replicas = draw_replicas(jax.random.fold_in(key_of[9], 71), 0)
    degree = plant(jax.random.randint(key_of[4], (NM,), K * TILE // 64, K * TILE // 16), jax.random.fold_in(key_of[4], 1), K * TILE // 64, (K * TILE // 16) - 1).astype(jnp.int32)
    self_one = centred(key_of[5], (FIN, HID), FIN ** -0.5, 0.5)
    neigh_one = centred(key_of[6], (FIN, HID), (FIN // 16) ** -0.5, 2.0)
    self_two = centred(key_of[7], (HID, HID), HID ** -0.5, 0.375)
    neigh_two = centred(key_of[8], (HID, HID), (HID // 16) ** -0.5, 1.5)
    return dict(features=features, tile_mask=tile_mask, tile_cols=tile_cols, replicas=replicas, degree=degree, self_one=self_one, neigh_one=neigh_one, self_two=self_two, neigh_two=neigh_two)


def aggregate_part(operands):
    local_values, masks, columns = operands
    feature_row_block = local_values.shape[0]
    tiled = local_values.astype(jnp.float32).reshape(feature_row_block, TILES, TILE)
    selected = jnp.take(tiled, columns, axis=1)
    summed = jnp.einsum("fiku,ikvu->fiv", selected, masks.astype(jnp.float32))
    return summed.reshape(feature_row_block, ROWS)


def layer(value_rows, tile_mask, tile_cols, replicas, degree, w_self, w_neigh):
    feature_row_block = value_rows.shape[0]
    flattened_index = (replicas[0] * MAST + replicas[2]).astype(jnp.int32)
    mirror_values = jnp.take(value_rows, flattened_index, axis=1).reshape(feature_row_block, EDGE_PARTITIONS, MIRROR_VERTICES)
    local_values = jnp.concatenate([value_rows.reshape(feature_row_block, EDGE_PARTITIONS, MAST), mirror_values], axis=2)
    partial_sum = lax.map(aggregate_part, (jnp.moveaxis(local_values, 1, 0), tile_mask.reshape(EDGE_PARTITIONS, TILES, K, TILE, TILE), tile_cols.reshape(EDGE_PARTITIONS, TILES, K)))
    own_part = jnp.moveaxis(partial_sum[:, :, :MAST], 0, 1).reshape(feature_row_block, EDGE_PARTITIONS * MAST)
    rounded_down = lax.optimization_barrier(partial_sum[:, :, MAST:].astype(jnp.bfloat16)).astype(jnp.float32)
    mirror_partition = jnp.moveaxis(rounded_down, 0, 1).reshape(feature_row_block, EDGE_PARTITIONS * MIRROR_VERTICES)
    total = own_part.at[:, flattened_index].add(mirror_partition)
    neighbours = (total / degree.astype(jnp.float32)[None, :]).astype(jnp.bfloat16)
    return jnp.dot(w_self.T, value_rows, preferred_element_type=jnp.float32) + jnp.dot(w_neigh.T, neighbours, preferred_element_type=jnp.float32)


def reference(features, tile_mask, tile_cols, replicas, degree, self_one, neigh_one, self_two, neigh_two):
    first = layer(features, tile_mask, tile_cols, replicas, degree, self_one, neigh_one)
    hidden = jax.nn.relu(first).astype(jnp.bfloat16)
    second = layer(hidden, tile_mask, tile_cols, replicas, degree, self_two, neigh_two)
    return second.astype(jnp.bfloat16)
```

```python
import functools

import jax
import jax.numpy as jnp
from jax import lax
from jax.experimental import pallas as pl
from jax.experimental.pallas import tpu as pltpu
from jax.sharding import PartitionSpec as P

F32 = jnp.float32
BF16 = jnp.bfloat16
I32 = jnp.int32
LANES = 128
CHUNK = 256
GROUP = 8
VMEM = pl.BlockSpec(memory_space=pltpu.VMEM)
SMEM = pl.BlockSpec(memory_space=pltpu.SMEM)


def call(body, out_shape, operands, smem=(), scratch=(), flops=0, moved=0):
    return pl.pallas_call(
        body,
        out_shape=out_shape,
        in_specs=[SMEM if i in smem else VMEM for i in range(len(operands))],
        out_specs=jax.tree.map(lambda _: VMEM, out_shape),
        scratch_shapes=list(scratch),
        compiler_params=pltpu.CompilerParams(vmem_limit_bytes=24 << 20),
        cost_estimate=pl.CostEstimate(flops=flops, bytes_accessed=moved, transcendentals=0),
    )(*operands)


def dot(left, right, dims=(1, 0)):
    return lax.dot_general(
        left, right, (((dims[0],), (dims[1],)), ((), ())), preferred_element_type=F32
    )


def one_hot(index_row, depth):
    rows = lax.broadcasted_iota(I32, (depth, index_row.shape[1]), 0)
    return (rows == index_row).astype(F32).astype(BF16)


def keep(condition, values):
    return jnp.where(condition, values, jnp.zeros_like(values))


def transpose_masks(tile_mask):
    tiles, stored, side, _ = tile_mask.shape
    step = max(d for d in (1, 2, 3, 4) if tiles % d == 0)

    def body(mask, out):
        for i in range(step):
            for k in range(stored):
                block = mask[i, k].astype(F32).T
                out[i, k * side : (k + 1) * side, :] = block.astype(BF16)

    return pl.pallas_call(
        body,
        grid=(tiles // step,),
        in_specs=[pl.BlockSpec((step, stored, side, side), lambda i: (i, 0, 0, 0))],
        out_specs=pl.BlockSpec((step, stored * side, side), lambda i: (i, 0, 0)),
        out_shape=jax.ShapeDtypeStruct((tiles, stored * side, side), BF16),
        compiler_params=pltpu.CompilerParams(vmem_limit_bytes=24 << 20),
        cost_estimate=pl.CostEstimate(flops=0, bytes_accessed=tile_mask.size * 6, transcendentals=0),
    )(tile_mask)


def slot_rows_body(dom, reps, out):
    capacity = out.shape[1]
    part, slot, row = reps[0:1, :], reps[1:2, :], reps[2:3, :]
    parts = lax.broadcasted_iota(I32, (dom, part.shape[1]), 0)
    mine = parts == part
    high = keep(mine, jnp.broadcast_to(row // CHUNK, mine.shape)).astype(F32).astype(BF16)
    low = keep(mine, jnp.broadcast_to(row % CHUNK, mine.shape)).astype(F32).astype(BF16)
    slots = one_hot(slot, capacity)
    rows = dot(high, slots, (1, 1)) * CHUNK + dot(low, slots, (1, 1))
    out[...] = rows.astype(I32)


def pick_part(groups, part, n, products):
    def one(g, total):
        found = products(g)
        for k in range(GROUP):
            total = total + keep(part == g * GROUP + k, found[k])
        return total

    return one


def partial_body(dom, dense, cols, received, own, masks, reps, own_out, out, local, mirror):
    feats = own.shape[0]
    masters = own.shape[1]
    mirrors = reps.shape[1]
    depth = received.shape[2]
    capacity = out.shape[2]
    tiles = masks.shape[0]
    stored = masks.shape[1] // LANES
    head = masters // LANES
    for i in range(head):
        local[i] = own[:, i * LANES : (i + 1) * LANES]
    for n in range(0, mirrors, CHUNK):
        part = reps[0:1, n : n + CHUNK]
        places = one_hot(reps[2:3, n : n + CHUNK] if dense else reps[1:2, n : n + CHUNK], depth)

        def add_group(g, total):
            block = received[pl.ds(g * GROUP, GROUP)].reshape(GROUP * feats, depth)
            found = dot(block, places).reshape(GROUP, feats, CHUNK)
            for k in range(GROUP):
                total = total + keep(part == g * GROUP + k, found[k])
            return total

        zero = jnp.zeros((feats, CHUNK), F32)
        if dom == GROUP:
            values = add_group(0, zero)
        else:
            values = lax.fori_loop(0, dom // GROUP, add_group, zero)
        for i in range(CHUNK // LANES):
            local[head + n // LANES + i] = values[:, i * LANES : (i + 1) * LANES].astype(BF16)
    for i in range(tiles):
        chosen = jnp.concatenate([local[cols[k, i]] for k in range(stored)], axis=1)
        summed = dot(chosen, masks[i])
        if i < head:
            own_out[:, i * LANES : (i + 1) * LANES] = summed
        else:
            at = (i - head) * LANES
            mirror[:, at : at + LANES] = summed.astype(BF16)
    slots = one_hot(reps[1:2, :], capacity)
    values = mirror[...].astype(F32)
    part = reps[0:1, :]

    def send_group(g, carry):
        spread = jnp.concatenate(
            [keep(part == g * GROUP + k, values).astype(BF16) for k in range(GROUP)], axis=0
        )
        placed = dot(spread, slots, (1, 1)).astype(BF16)
        out[pl.ds(g * GROUP, GROUP)] = placed.reshape(GROUP, feats, capacity)
        return carry

    if dom == GROUP:
        send_group(0, 0)
    else:
        lax.fori_loop(0, dom // GROUP, send_group, 0)


def partial_sums(dom, dense, cols, received, own, masks, reps, capacity):
    feats, masters = own.shape
    mirrors = reps.shape[1]
    tiles = masks.shape[0]
    return call(
        functools.partial(partial_body, dom, dense),
        (
            jax.ShapeDtypeStruct((feats, masters), F32),
            jax.ShapeDtypeStruct((dom, feats, capacity), BF16),
        ),
        (cols, received, own, masks, reps),
        smem=(0,),
        scratch=(pltpu.VMEM((tiles, feats, LANES), BF16), pltpu.VMEM((feats, mirrors), BF16)),
        flops=2 * feats * masks.size,
        moved=2 * masks.size,
    )


def mean_body(dom, received, rows, own, degree, out):
    feats, masters = own.shape
    parts = masters // CHUNK

    def add(p, total):
        row = rows[pl.ds(p, 1), :]
        values = received[p].astype(F32)
        high = row // CHUNK
        spread = jnp.concatenate([keep(high == a, values).astype(BF16) for a in range(parts)], axis=0)
        return total + dot(spread, one_hot(row % CHUNK, CHUNK), (1, 1))

    total = jnp.zeros((parts * feats, CHUNK), F32)
    if dom == GROUP:
        for p in range(dom):
            total = add(p, total)
    else:
        total = lax.fori_loop(0, dom, add, total)
    for a in range(parts):
        at = slice(a * CHUNK, (a + 1) * CHUNK)
        whole = own[:, at] + total[a * feats : (a + 1) * feats]
        out[:, at] = (whole / degree[:, at].astype(F32)).astype(BF16)


def mean(dom, received, rows, own, degree):
    feats, masters = own.shape
    return call(
        functools.partial(mean_body, dom),
        jax.ShapeDtypeStruct((feats, masters), BF16),
        (received, rows, own, degree),
        flops=2 * received.size * masters,
        moved=received.size * 2,
    )


def serve_body(dom, self_t, neigh_t, inputs, means, rows, hidden_out, out):
    result = dot(self_t[...], inputs[...]) + dot(neigh_t[...], means[...])
    hidden = jnp.maximum(result, 0.0).astype(BF16)
    hidden_out[...] = hidden
    feats, masters = hidden.shape
    parts = masters // CHUNK
    folded = jnp.concatenate([hidden[:, a * CHUNK : (a + 1) * CHUNK] for a in range(parts)], axis=0)

    def one(p, carry):
        row = rows[pl.ds(p, 1), :]
        found = dot(folded, one_hot(row % CHUNK, CHUNK))
        high = row // CHUNK
        total = jnp.zeros((feats, row.shape[1]), F32)
        for a in range(parts):
            total = total + keep(high == a, found[a * feats : (a + 1) * feats])
        out[p] = total.astype(BF16)
        return carry

    if dom == GROUP:
        for p in range(dom):
            one(p, 0)
    else:
        lax.fori_loop(0, dom, one, 0)


def serve(dom, self_t, neigh_t, inputs, means, rows):
    feats = self_t.shape[0]
    masters = inputs.shape[1]
    capacity = rows.shape[1]
    return call(
        functools.partial(serve_body, dom),
        (
            jax.ShapeDtypeStruct((feats, masters), BF16),
            jax.ShapeDtypeStruct((dom, feats, capacity), BF16),
        ),
        (self_t, neigh_t, inputs, means, rows),
        flops=2 * feats * masters * dom * capacity,
        moved=2 * feats * dom * capacity,
    )


def self_body(self_one_t, neigh_one_t, self_two_t, inputs, means, out):
    result = dot(self_one_t[...], inputs[...]) + dot(neigh_one_t[...], means[...])
    hidden = jnp.maximum(result, 0.0).astype(BF16)
    out[...] = dot(self_two_t[...], hidden)


def embed_body(neigh_two_t, means, own, out):
    out[...] = (own[...] + dot(neigh_two_t[...], means[...])).astype(BF16)


def on_device(
    features, tile_mask, tile_cols, replicas, degree, self_one, neigh_one, self_two, neigh_two
):
    dom = lax.axis_size("dom")
    feat = lax.axis_size("feat")
    masters = features.shape[1]
    mirrors = replicas.shape[1]
    capacity = -(-(2 * mirrors // dom) // LANES) * LANES
    cols = tile_cols.T
    degree = degree.reshape(1, masters)

    def exchange(blocks):
        return lax.all_to_all(blocks, "dom", split_axis=0, concat_axis=0, tiled=True)

    def own_rows(weights):
        width = weights.shape[1] // feat
        start = lax.axis_index("feat") * width
        return lax.dynamic_slice_in_dim(weights, start, width, 1).T

    spread = exchange(jnp.broadcast_to(features[None], (dom,) + features.shape))
    slot_rows = call(
        functools.partial(slot_rows_body, dom),
        jax.ShapeDtypeStruct((dom, capacity), I32),
        (replicas,),
        flops=4 * dom * mirrors * capacity,
        moved=12 * mirrors,
    )
    rows = exchange(slot_rows)
    whole_in = lax.all_gather(features, "feat", axis=0, tiled=True)
    masks = transpose_masks(tile_mask)
    self_one_t, neigh_one_t = own_rows(self_one), own_rows(neigh_one)
    self_two_t, neigh_two_t = own_rows(self_two), own_rows(neigh_two)

    own_one, outgoing_one = partial_sums(
        dom, True, cols, spread, features, masks, replicas, capacity
    )
    mean_one = mean(dom, exchange(outgoing_one), rows, own_one, degree)
    whole_one = lax.all_gather(mean_one, "feat", axis=0, tiled=True)
    hidden, asked = serve(dom, self_one_t, neigh_one_t, whole_in, whole_one, rows)
    hidden_mirrors = exchange(asked)
    self_part = call(
        self_body,
        jax.ShapeDtypeStruct((self_two_t.shape[0], masters), F32),
        (self_one.T, neigh_one.T, self_two_t, whole_in, whole_one),
        flops=2 * masters * (2 * self_one.size + self_two_t.size),
        moved=masters * 1024,
    )
    own_two, outgoing_two = partial_sums(
        dom, False, cols, hidden_mirrors, hidden, masks, replicas, capacity
    )
    mean_two = mean(dom, exchange(outgoing_two), rows, own_two, degree)
    whole_two = lax.all_gather(mean_two, "feat", axis=0, tiled=True)
    return call(
        embed_body,
        jax.ShapeDtypeStruct((neigh_two_t.shape[0], masters), BF16),
        (neigh_two_t, whole_two, self_part),
        flops=2 * masters * neigh_two_t.size,
        moved=masters * 1024,
    )


def solution(mesh):
    return jax.shard_map(
        on_device,
        mesh=mesh,
        in_specs=(
            P("feat", "dom"),
            P("dom", None, None, None),
            P("dom", None),
            P(None, "dom"),
            P("dom"),
            P(),
            P(),
            P(),
            P(),
        ),
        out_specs=P("feat", "dom"),
        check_vma=False,
    )
```

```python
import functools

import jax
import jax.numpy as jnp
from jax import lax
from jax.experimental import pallas as pl
from jax.experimental.pallas import tpu as pltpu
from jax.sharding import PartitionSpec as P

F32 = jnp.float32
BF16 = jnp.bfloat16
I32 = jnp.int32
MASK = jnp.float8_e4m3fn
LANES = 128
SHIFT = 8
CHUNK = 1 << SHIFT
GROUP = 8
ORDER = (5, 2, 3, 7, 1, 0, 4, 6)
INDEX_ROWS = 16
VMEM = pl.BlockSpec(memory_space=pltpu.VMEM)
SMEM = pl.BlockSpec(memory_space=pltpu.SMEM)
HBM = pl.BlockSpec(memory_space=pltpu.HBM)
PIECES = 4
MASK_PIECES = 8
SPARE = 10


def call(body, out_shape, operands, smem=(), hbm=(), hbm_out=(), scratch=(), flops=0, moved=0, limit=20):
    def place(i):
        return SMEM if i in smem else HBM if i in hbm else VMEM

    return pl.pallas_call(
        body,
        out_shape=out_shape,
        in_specs=[place(i) for i in range(len(operands))],
        out_specs=(
            tuple(HBM if i in hbm_out else VMEM for i in range(len(out_shape)))
            if isinstance(out_shape, tuple)
            else VMEM
        ),
        scratch_shapes=list(scratch),
        compiler_params=pltpu.CompilerParams(vmem_limit_bytes=limit << 20),
        cost_estimate=pl.CostEstimate(flops=flops, bytes_accessed=moved, transcendentals=0),
    )(*operands)


def dot(left, right, dims=(1, 0)):
    return lax.dot_general(
        left, right, (((dims[0],), (dims[1],)), ((), ())), preferred_element_type=F32
    )


def one_hot(index_row, depth):
    side = min(depth, CHUNK)
    n = index_row.shape[1]
    rows = lax.broadcasted_iota(I32, (side, n), 0).astype(F32).astype(BF16)
    blocks = []
    for start in range(0, depth, side):
        here = (index_row >= start) & (index_row < start + side)
        spot = jnp.where(here, index_row - start, -1).astype(F32).astype(BF16)
        blocks.append(jnp.where(rows == spot, jnp.ones_like(rows), jnp.zeros_like(rows)))
    return blocks[0] if len(blocks) == 1 else jnp.concatenate(blocks, axis=0)


def keep(condition, values):
    return jnp.where(condition, values, jnp.zeros_like(values))


def loop(count, body, carry):
    if count <= GROUP:
        for i in range(count):
            carry = body(i, carry)
        return carry
    return lax.fori_loop(0, count, body, carry)


def masks_body(tile_mask, out, blocks, arrived):
    tiles, stored, side, _ = blocks.shape
    copies = fetch(tile_mask, blocks, arrived)
    step = tiles // len(copies)
    for i in range(tiles):
        if i % step == 0:
            copies[i // step].wait()
        for k in range(stored):
            block = blocks[i, k].astype(F32).astype(BF16)
            out[i, k * side : (k + 1) * side, :] = block.T


def transpose_masks(tile_mask):
    tiles, stored, side, _ = tile_mask.shape
    return call(
        masks_body,
        jax.ShapeDtypeStruct((tiles, stored * side, side), BF16),
        (tile_mask,),
        hbm=(0,),
        limit=47,
        scratch=(
            pltpu.VMEM(tile_mask.shape, I32),
            pltpu.SemaphoreType.DMA((MASK_PIECES,)),
        ),
        moved=6 * tile_mask.size,
    )


def index_rows(part, row, slot_places, names):
    blocks = slot_places.shape[0] // LANES
    name = lax.broadcasted_iota(I32, (len(names), 1), 0)
    for k, q in enumerate(names):
        name = jnp.where(lax.broadcasted_iota(I32, (len(names), 1), 0) == k, q, name)
    mine = jnp.broadcast_to(name, (len(names), part.shape[1])) == part
    digits = [keep(mine, jnp.broadcast_to(d, mine.shape)) for d in (row >> SHIFT, row & (CHUNK - 1))]
    digits = jnp.concatenate(digits, axis=0).astype(F32).astype(BF16)
    found = dot(digits, slot_places, (1, 1))
    out = []
    for k in range(len(names)):
        pieces = [
            found[at : at + 1, b * LANES : (b + 1) * LANES]
            for at in (k, len(names) + k)
            for b in range(blocks)
        ]
        pieces.append(jnp.zeros((INDEX_ROWS - len(pieces), LANES), F32))
        out.append(jnp.concatenate(pieces, axis=0).astype(BF16))
    return out


def pick(blocks, names, spots, part, feats):
    found = dot(jnp.concatenate(blocks, axis=0), spots)
    total = jnp.zeros((feats, spots.shape[1]), F32)
    for k, name in enumerate(names):
        total = total + keep(part == name, found[k * feats : (k + 1) * feats])
    return total


def pick_all(order, received, spots, part, feats):
    dom = received.shape[0]
    if dom == GROUP:
        return pick([received[k] for k in range(dom)], order, spots, part, feats)

    def add_group(g, total):
        blocks = [received[g * GROUP + k] for k in range(GROUP)]
        return total + pick(blocks, range(GROUP), spots, part - g * GROUP, feats)

    return lax.fori_loop(0, dom // GROUP, add_group, jnp.zeros((feats, spots.shape[1]), F32))


def fetch(source, target, arrived):
    pieces = arrived.shape[0]
    step = target.shape[0] // pieces
    copies = []
    for i in range(pieces):
        at = pl.ds(i * step, step)
        copies.append(pltpu.make_async_copy(source.at[at], target.at[at], arrived.at[i]))
        copies[-1].start()
    return copies


def aggregate(cols, local, masks, head, own_out, mirror, narrow=None):
    stored = masks.shape[1] // LANES
    for i in range(masks.shape[0]):
        chosen = jnp.concatenate([local[cols[k, i]] for k in range(stored)], axis=1)
        row = masks[i]
        if narrow is not None:
            narrow[i] = row.astype(MASK)
        summed = dot(chosen, row.astype(BF16))
        if i < head:
            own_out[:, i * LANES : (i + 1) * LANES] = summed
        else:
            at = (i - head) * LANES
            mirror[:, at : at + LANES] = summed.astype(BF16)


def send(order, mirror, reps, out, with_index):
    feats = mirror.shape[0]
    dom = out.shape[0]
    rows = out.shape[1] // feats * feats
    blocks = rows // feats
    part, slot, row = reps[0:1, :], reps[1:2, :], reps[2:3, :]
    slot_places = one_hot(slot, blocks * LANES)
    values = mirror[...]

    def group(first, names, part):
        spread = jnp.concatenate([keep(part == name, values) for name in names], axis=0)
        placed = dot(spread, slot_places, (1, 1)).astype(BF16)
        for k in range(GROUP):
            for b in range(blocks):
                block = placed[k * feats : (k + 1) * feats, b * LANES : (b + 1) * LANES]
                out[first + k, b * feats : (b + 1) * feats, :] = block
        if with_index:
            for k, index in enumerate(index_rows(part, row, slot_places, names)):
                out[first + k, rows:, :] = index

    if dom == GROUP:
        group(0, order, part)
    else:

        def one(g, carry):
            group(g * GROUP, range(GROUP), part - g * GROUP)
            return carry

        lax.fori_loop(0, dom // GROUP, one, 0)


def first_body(order, cols, own, masks, reps, *refs):
    received = refs[:-8]
    own_out, all_out, out, kept, local, mirror, narrow, written = refs[-8:]
    feats, masters = own.shape
    head = masters // LANES
    for i in range(head):
        local[i] = own[:, i * LANES : (i + 1) * LANES]
    for n in range(0, reps.shape[1], CHUNK):
        at = slice(n, n + CHUNK)
        spots = one_hot(reps[2:3, at], masters)
        part = reps[0:1, at]
        if len(received) == 1:
            values = pick_all(order, received[0], spots, part, feats)
        else:
            part = part ^ lax.axis_index("dom")
            blocks = [ref[...] for ref in received]
            values = pick(blocks, range(1, len(blocks) + 1), spots, part, feats)
        values = values.astype(BF16)
        all_out[:, at] = values
        for i in range(CHUNK // LANES):
            local[head + n // LANES + i] = values[:, i * LANES : (i + 1) * LANES]
    aggregate(cols, local, masks, head, own_out, mirror, narrow)
    copy = pltpu.make_async_copy(narrow, kept.at[pl.ds(0, masks.shape[0])], written)
    copy.start()
    send(order, mirror, reps, out, True)
    copy.wait()


def first_sums(order, cols, received, own, masks, reps, capacity):
    feats, masters = own.shape
    mirrors = reps.shape[1]
    rows = capacity // LANES * feats + INDEX_ROWS
    tiles = masks.shape[0]
    return call(
        functools.partial(first_body, order),
        (
            jax.ShapeDtypeStruct((feats, masters), F32),
            jax.ShapeDtypeStruct((feats, mirrors), BF16),
            jax.ShapeDtypeStruct((len(order), rows, LANES), BF16),
            jax.ShapeDtypeStruct((SPARE * tiles,) + masks.shape[1:], MASK),
        ),
        (cols, own, masks, reps) + received,
        smem=(0,),
        hbm_out=(3,),
        limit=44,
        scratch=(
            pltpu.VMEM((tiles, feats, LANES), BF16),
            pltpu.VMEM((feats, mirrors), BF16),
            pltpu.VMEM(masks.shape, MASK),
            pltpu.SemaphoreType.DMA,
        ),
        flops=2 * feats * masks.size,
        moved=2 * masks.size,
    )


def message(received, p, feats, blocks):
    return jnp.concatenate([received[p, b * feats : (b + 1) * feats, :] for b in range(blocks)], axis=1)


def add_mirrors(dom, received, high, low, feats, blocks, masters):
    parts = masters // CHUNK

    def add(p, total):
        values = message(received, p, feats, blocks)
        spread = jnp.concatenate([keep(high(p) == a, values) for a in range(parts)], axis=0)
        return total + dot(spread, one_hot(low(p), CHUNK), (1, 1))

    return loop(dom, add, jnp.zeros((parts * feats, CHUNK), F32))


def divide(total, own, degree, out):
    feats, masters = own.shape
    for a in range(masters // CHUNK):
        at = slice(a * CHUNK, (a + 1) * CHUNK)
        whole = own[:, at] + total[a * feats : (a + 1) * feats]
        out[:, at] = (whole / degree[:, at].astype(F32)).astype(BF16)


def first_mean_body(received, features, own, degree, out, asked, rows_out, mean):
    feats, masters = own.shape
    dom, capacity = rows_out.shape
    blocks = capacity // LANES
    parts = masters // CHUNK

    def rows(p, carry):
        coded = received[p, blocks * feats :, :].astype(F32).astype(I32)
        high = jnp.concatenate([coded[b : b + 1] for b in range(blocks)], axis=1)
        low = jnp.concatenate([coded[blocks + b : blocks + b + 1] for b in range(blocks)], axis=1)
        rows_out[pl.ds(p, 1), :] = high * CHUNK + low
        return carry

    loop(dom, rows, 0)

    def high(p):
        return rows_out[pl.ds(p, 1), :] >> SHIFT

    def low(p):
        return rows_out[pl.ds(p, 1), :] & (CHUNK - 1)

    total = add_mirrors(dom, received, high, low, feats, blocks, masters)
    divide(total, own, degree, mean)
    folded = jnp.concatenate([mean[:, a * CHUNK : (a + 1) * CHUNK] for a in range(parts)], axis=0)

    def one(p, carry):
        found = dot(folded, one_hot(low(p), CHUNK))
        chosen = jnp.zeros((feats, capacity), F32)
        for a in range(parts):
            chosen = chosen + keep(high(p) == a, found[a * feats : (a + 1) * feats])
        asked[p] = chosen.astype(BF16)
        return carry

    loop(dom, one, 0)
    out[:feats] = features[...]
    out[feats:] = mean[...]


def first_mean(dom, received, features, own, degree, capacity):
    feats, masters = own.shape
    return call(
        first_mean_body,
        (
            jax.ShapeDtypeStruct((2 * feats, masters), BF16),
            jax.ShapeDtypeStruct((dom, feats, capacity), BF16),
            jax.ShapeDtypeStruct((dom, capacity), I32),
        ),
        (received, features, own, degree),
        scratch=(pltpu.VMEM((feats, masters), BF16),),
        flops=2 * received.size * masters,
        moved=received.size * 2,
    )


def collect_body(order, received, reps, masks_hbm, out, masks, arrived):
    copies = fetch(masks_hbm, masks, arrived)
    feats = out.shape[0]
    for n in range(0, reps.shape[1], CHUNK):
        at = slice(n, n + CHUNK)
        spots = one_hot(reps[1:2, at], received.shape[2])
        out[:, at] = pick_all(order, received, spots, reps[0:1, at], feats).astype(BF16)
    for copy in copies:
        copy.wait()


def hidden_body(weights_t, own_t, self_own_t, self_two_own, inputs, mirrors, own_out, mirror_out, self_out):
    own_out[...] = jnp.maximum(dot(own_t[...], inputs[...]), 0.0).astype(BF16)
    mirror_out[...] = dot(self_own_t[...], mirrors[...])
    hidden = jnp.maximum(dot(weights_t[...], inputs[...]), 0.0).astype(BF16)
    self_out[...] = dot(self_two_own[...], hidden)


def second_body(order, cols, means, mirror_self, neigh_t, own, masks, reps, own_out, out, local, mirror):
    feats, masters = own.shape
    head = masters // LANES
    for i in range(head):
        local[i] = own[:, i * LANES : (i + 1) * LANES]
    for n in range(0, reps.shape[1], CHUNK):
        at = slice(n, n + CHUNK)
        result = mirror_self[:, at] + dot(neigh_t[...], means[:, at])
        values = jnp.maximum(result, 0.0).astype(BF16)
        for i in range(CHUNK // LANES):
            local[head + n // LANES + i] = values[:, i * LANES : (i + 1) * LANES]
    aggregate(cols, local, masks, head, own_out, mirror)
    send(order, mirror, reps, out, False)


def second_sums(order, cols, means, mirror_self, neigh_t, own, masks, reps, capacity):
    feats, masters = own.shape
    mirrors = reps.shape[1]
    rows = capacity // LANES * feats
    return call(
        functools.partial(second_body, order),
        (
            jax.ShapeDtypeStruct((feats, masters), F32),
            jax.ShapeDtypeStruct((len(order), rows, LANES), BF16),
        ),
        (cols, means, mirror_self, neigh_t, own, masks, reps),
        smem=(0,),
        scratch=(
            pltpu.VMEM((masks.shape[0], feats, LANES), BF16),
            pltpu.VMEM((feats, mirrors), BF16),
        ),
        flops=2 * feats * masks.size,
        moved=masks.size,
    )


def second_mean_body(received, rows, own, degree, out):
    feats, masters = own.shape
    dom, capacity = rows.shape

    def high(p):
        return rows[pl.ds(p, 1), :] >> SHIFT

    def low(p):
        return rows[pl.ds(p, 1), :] & (CHUNK - 1)

    total = add_mirrors(dom, received, high, low, feats, capacity // LANES, masters)
    divide(total, own, degree, out)


def embed_body(neigh_t, means, own, out):
    out[...] = (own[...] + dot(neigh_t[...], means[...])).astype(BF16)


def on_device(
    features, tile_mask, tile_cols, replicas, degree, self_one, neigh_one, self_two, neigh_two
):
    dom = lax.axis_size("dom")
    feat = lax.axis_size("feat")
    feats, masters = features.shape
    mirrors = replicas.shape[1]
    hidden_feats = self_one.shape[1] // feat
    capacity = -(-(2 * mirrors // dom) // LANES) * LANES
    cols = tile_cols.T
    degree = degree.reshape(1, masters)

    order = ORDER if dom == len(ORDER) else tuple(range(dom))

    def exchange(blocks):
        return lax.all_to_all(
            blocks, "dom", split_axis=0, concat_axis=0, tiled=True, axis_index_groups=[list(order)]
        )

    def gather(rows):
        return lax.all_gather(rows, "feat", axis=0, tiled=True)

    def own_rows(weights):
        width = weights.shape[1] // feat
        start = lax.axis_index("feat") * width
        return lax.dynamic_slice_in_dim(weights, start, width, 1).T

    def spread(columns):
        if dom != GROUP:
            return (exchange(jnp.broadcast_to(columns[None], (dom,) + columns.shape)),)
        half = dom // 2
        others = list(range(1, half))

        def swap(values, k):
            return lax.ppermute(values, "dom", [(i, i ^ k) for i in range(dom)])

        far = swap(columns, half)
        near = [swap(columns, k) for k in others]
        return (*near, far, *[swap(far, k) for k in others])

    both = jnp.concatenate(
        [self_one.reshape(feat, feats, -1), neigh_one.reshape(feat, feats, -1)], axis=1
    ).reshape(2 * feat * feats, -1)
    self_one_own, neigh_one_own, both_own = own_rows(self_one), own_rows(neigh_one), own_rows(both)
    self_two_own, neigh_two_own = own_rows(self_two), own_rows(neigh_two)

    received = spread(features)
    masks = transpose_masks(tile_mask)
    own_one, mirror_in, outgoing, kept_masks = first_sums(
        order, cols, received, features, masks, replicas, capacity
    )
    sums, mirror_in = lax.optimization_barrier((exchange(outgoing), gather(mirror_in)))
    own_both, asked, rows = first_mean(dom, sums, features, own_one, degree, capacity)
    slots = exchange(asked)
    hidden, mirror_self, self_part = call(
        hidden_body,
        (
            jax.ShapeDtypeStruct((hidden_feats, masters), BF16),
            jax.ShapeDtypeStruct((hidden_feats, mirrors), F32),
            jax.ShapeDtypeStruct((self_two_own.shape[0], masters), F32),
        ),
        (both.T, both_own, self_one_own, self_two_own, gather(own_both), mirror_in),
        flops=2 * masters * (4 * self_one.size + self_two_own.size),
        moved=masters * 1024,
    )
    mirror_mean, near_masks = call(
        functools.partial(collect_body, order),
        (
            jax.ShapeDtypeStruct((feats, mirrors), BF16),
            jax.ShapeDtypeStruct(masks.shape, MASK),
        ),
        (slots, replicas, kept_masks),
        hbm=(2,),
        limit=44,
        scratch=(pltpu.SemaphoreType.DMA((PIECES,)),),
        flops=2 * slots.size * mirrors,
        moved=2 * slots.size,
    )
    own_two, outgoing = second_sums(
        order, cols, gather(mirror_mean), mirror_self, neigh_one_own, hidden, near_masks, replicas, capacity
    )
    mean_two = call(
        second_mean_body,
        jax.ShapeDtypeStruct((hidden_feats, masters), BF16),
        (exchange(outgoing), rows, own_two, degree),
        flops=2 * hidden_feats * dom * capacity * masters,
        moved=2 * hidden_feats * dom * capacity,
    )
    return call(
        embed_body,
        jax.ShapeDtypeStruct((neigh_two_own.shape[0], masters), BF16),
        (neigh_two_own, gather(mean_two), self_part),
        flops=2 * masters * neigh_two_own.size,
        moved=masters * 1024,
    )


def solution(mesh):
    return jax.shard_map(
        on_device,
        mesh=mesh,
        in_specs=(
            P("feat", "dom"),
            P("dom", None, None, None),
            P("dom", None),
            P(None, "dom"),
            P("dom"),
            P(),
            P(),
            P(),
            P(),
        ),
        out_specs=P("feat", "dom"),
        check_vma=False,
    )
```

```python
import functools

import jax
import jax.numpy as jnp
from jax import lax
from jax.experimental import pallas as pl
from jax.experimental.pallas import tpu as pltpu
from jax.sharding import PartitionSpec as P

F32 = jnp.float32
BF16 = jnp.bfloat16
I32 = jnp.int32
MASK = jnp.float8_e4m3fn
LANES = 128
SHIFT = 8
CHUNK = 1 << SHIFT
GROUP = 8
ORDER = (4, 7, 2, 6, 1, 0, 5, 3)
INDEX_ROWS = 16
VMEM = pl.BlockSpec(memory_space=pltpu.VMEM)
SMEM = pl.BlockSpec(memory_space=pltpu.SMEM)
HBM = pl.BlockSpec(memory_space=pltpu.HBM)
PIECES = 4
MASK_PIECES = 8
SPARE = 10


def call(body, out_shape, operands, smem=(), hbm=(), hbm_out=(), scratch=(), flops=0, moved=0, limit=20):
    def place(i):
        return SMEM if i in smem else HBM if i in hbm else VMEM

    return pl.pallas_call(
        body,
        out_shape=out_shape,
        in_specs=[place(i) for i in range(len(operands))],
        out_specs=(
            tuple(HBM if i in hbm_out else VMEM for i in range(len(out_shape)))
            if isinstance(out_shape, tuple)
            else VMEM
        ),
        scratch_shapes=list(scratch),
        compiler_params=pltpu.CompilerParams(vmem_limit_bytes=limit << 20),
        cost_estimate=pl.CostEstimate(flops=flops, bytes_accessed=moved, transcendentals=0),
    )(*operands)


def dot(left, right, dims=(1, 0)):
    return lax.dot_general(
        left, right, (((dims[0],), (dims[1],)), ((), ())), preferred_element_type=F32
    )


def one_hot(index_row, depth):
    side = min(depth, CHUNK)
    n = index_row.shape[1]
    rows = lax.broadcasted_iota(I32, (side, n), 0).astype(F32).astype(BF16)
    blocks = []
    for start in range(0, depth, side):
        here = (index_row >= start) & (index_row < start + side)
        spot = jnp.where(here, index_row - start, -1).astype(F32).astype(BF16)
        blocks.append(jnp.where(rows == spot, jnp.ones_like(rows), jnp.zeros_like(rows)))
    return blocks[0] if len(blocks) == 1 else jnp.concatenate(blocks, axis=0)


def keep(condition, values):
    return jnp.where(condition, values, jnp.zeros_like(values))


def loop(count, body, carry):
    if count <= GROUP:
        for i in range(count):
            carry = body(i, carry)
        return carry
    return lax.fori_loop(0, count, body, carry)


def masks_body(tile_mask, out, blocks, arrived):
    tiles, stored, side, _ = blocks.shape
    copies = fetch(tile_mask, blocks, arrived)
    step = tiles // len(copies)
    for i in range(tiles):
        if i % step == 0:
            copies[i // step].wait()
        for k in range(stored):
            block = blocks[i, k].astype(F32).astype(BF16)
            out[i, k * side : (k + 1) * side, :] = block.T


def transpose_masks(tile_mask):
    tiles, stored, side, _ = tile_mask.shape
    return call(
        masks_body,
        jax.ShapeDtypeStruct((tiles, stored * side, side), BF16),
        (tile_mask,),
        hbm=(0,),
        limit=47,
        scratch=(
            pltpu.VMEM(tile_mask.shape, I32),
            pltpu.SemaphoreType.DMA((MASK_PIECES,)),
        ),
        moved=6 * tile_mask.size,
    )


def index_rows(part, row, slot_places, names):
    blocks = slot_places.shape[0] // LANES
    name = lax.broadcasted_iota(I32, (len(names), 1), 0)
    for k, q in enumerate(names):
        name = jnp.where(lax.broadcasted_iota(I32, (len(names), 1), 0) == k, q, name)
    mine = jnp.broadcast_to(name, (len(names), part.shape[1])) == part
    digits = [keep(mine, jnp.broadcast_to(d, mine.shape)) for d in (row >> SHIFT, row & (CHUNK - 1))]
    digits = jnp.concatenate(digits, axis=0).astype(F32).astype(BF16)
    found = dot(digits, slot_places, (1, 1))
    out = []
    for k in range(len(names)):
        pieces = [
            found[at : at + 1, b * LANES : (b + 1) * LANES]
            for at in (k, len(names) + k)
            for b in range(blocks)
        ]
        pieces.append(jnp.zeros((INDEX_ROWS - len(pieces), LANES), F32))
        out.append(jnp.concatenate(pieces, axis=0).astype(BF16))
    return out


def pick(blocks, names, spots, part, feats):
    found = dot(jnp.concatenate(blocks, axis=0), spots)
    total = jnp.zeros((feats, spots.shape[1]), F32)
    for k, name in enumerate(names):
        total = total + keep(part == name, found[k * feats : (k + 1) * feats])
    return total


def pick_all(order, received, spots, part, feats):
    dom = received.shape[0]
    if dom == GROUP:
        return pick([received[k] for k in range(dom)], order, spots, part, feats)

    def add_group(g, total):
        blocks = [received[g * GROUP + k] for k in range(GROUP)]
        return total + pick(blocks, range(GROUP), spots, part - g * GROUP, feats)

    return lax.fori_loop(0, dom // GROUP, add_group, jnp.zeros((feats, spots.shape[1]), F32))


def fetch(source, target, arrived):
    pieces = arrived.shape[0]
    step = target.shape[0] // pieces
    copies = []
    for i in range(pieces):
        at = pl.ds(i * step, step)
        copies.append(pltpu.make_async_copy(source.at[at], target.at[at], arrived.at[i]))
        copies[-1].start()
    return copies


def aggregate(cols, local, masks, head, own_out, mirror, narrow=None):
    stored = masks.shape[1] // LANES
    for i in range(masks.shape[0]):
        chosen = jnp.concatenate([local[cols[k, i]] for k in range(stored)], axis=1)
        row = masks[i]
        if narrow is not None:
            narrow[i] = row.astype(MASK)
        summed = dot(chosen, row.astype(BF16))
        if i < head:
            own_out[:, i * LANES : (i + 1) * LANES] = summed
        else:
            at = (i - head) * LANES
            mirror[:, at : at + LANES] = summed.astype(BF16)


def send(order, mirror, reps, out, with_index):
    feats = mirror.shape[0]
    dom = out.shape[0]
    rows = out.shape[1] // feats * feats
    blocks = rows // feats
    part, slot, row = reps[0:1, :], reps[1:2, :], reps[2:3, :]
    slot_places = one_hot(slot, blocks * LANES)
    values = mirror[...]

    def group(first, names, part):
        spread = jnp.concatenate([keep(part == name, values) for name in names], axis=0)
        placed = dot(spread, slot_places, (1, 1)).astype(BF16)
        for k in range(GROUP):
            for b in range(blocks):
                block = placed[k * feats : (k + 1) * feats, b * LANES : (b + 1) * LANES]
                out[first + k, b * feats : (b + 1) * feats, :] = block
        if with_index:
            for k, index in enumerate(index_rows(part, row, slot_places, names)):
                out[first + k, rows:, :] = index

    if dom == GROUP:
        group(0, order, part)
    else:

        def one(g, carry):
            group(g * GROUP, range(GROUP), part - g * GROUP)
            return carry

        lax.fori_loop(0, dom // GROUP, one, 0)


def first_body(order, cols, own, masks, reps, *refs):
    received = refs[:-8]
    own_out, all_out, out, kept, local, mirror, narrow, written = refs[-8:]
    feats, masters = own.shape
    head = masters // LANES
    for i in range(head):
        local[i] = own[:, i * LANES : (i + 1) * LANES]
    for n in range(0, reps.shape[1], CHUNK):
        at = slice(n, n + CHUNK)
        spots = one_hot(reps[2:3, at], masters)
        part = reps[0:1, at]
        if len(received) == 1:
            values = pick_all(order, received[0], spots, part, feats)
        else:
            part = part ^ lax.axis_index("dom")
            blocks = [ref[...] for ref in received]
            values = pick(blocks, range(1, len(blocks) + 1), spots, part, feats)
        values = values.astype(BF16)
        all_out[:, at] = values
        for i in range(CHUNK // LANES):
            local[head + n // LANES + i] = values[:, i * LANES : (i + 1) * LANES]
    aggregate(cols, local, masks, head, own_out, mirror, narrow)
    copy = pltpu.make_async_copy(narrow, kept.at[pl.ds(0, masks.shape[0])], written)
    copy.start()
    send(order, mirror, reps, out, True)
    copy.wait()


def first_sums(order, cols, received, own, masks, reps, capacity):
    feats, masters = own.shape
    mirrors = reps.shape[1]
    rows = capacity // LANES * feats + INDEX_ROWS
    tiles = masks.shape[0]
    return call(
        functools.partial(first_body, order),
        (
            jax.ShapeDtypeStruct((feats, masters), F32),
            jax.ShapeDtypeStruct((feats, mirrors), BF16),
            jax.ShapeDtypeStruct((len(order), rows, LANES), BF16),
            jax.ShapeDtypeStruct((SPARE * tiles,) + masks.shape[1:], MASK),
        ),
        (cols, own, masks, reps) + received,
        smem=(0,),
        hbm_out=(3,),
        limit=44,
        scratch=(
            pltpu.VMEM((tiles, feats, LANES), BF16),
            pltpu.VMEM((feats, mirrors), BF16),
            pltpu.VMEM(masks.shape, MASK),
            pltpu.SemaphoreType.DMA,
        ),
        flops=2 * feats * masks.size,
        moved=2 * masks.size,
    )


def message(received, p, feats, blocks):
    return jnp.concatenate([received[p, b * feats : (b + 1) * feats, :] for b in range(blocks)], axis=1)


def add_mirrors(dom, received, high, low, feats, blocks, masters):
    parts = masters // CHUNK

    def add(p, total):
        values = message(received, p, feats, blocks)
        spread = jnp.concatenate([keep(high(p) == a, values) for a in range(parts)], axis=0)
        return total + dot(spread, one_hot(low(p), CHUNK), (1, 1))

    return loop(dom, add, jnp.zeros((parts * feats, CHUNK), F32))


def divide(total, own, degree, out):
    feats, masters = own.shape
    for a in range(masters // CHUNK):
        at = slice(a * CHUNK, (a + 1) * CHUNK)
        whole = own[:, at] + total[a * feats : (a + 1) * feats]
        out[:, at] = (whole / degree[:, at].astype(F32)).astype(BF16)


def first_mean_body(received, features, own, degree, out, asked, rows_out, mean):
    feats, masters = own.shape
    dom, capacity = rows_out.shape
    blocks = capacity // LANES
    parts = masters // CHUNK

    def rows(p, carry):
        coded = received[p, blocks * feats :, :].astype(F32).astype(I32)
        high = jnp.concatenate([coded[b : b + 1] for b in range(blocks)], axis=1)
        low = jnp.concatenate([coded[blocks + b : blocks + b + 1] for b in range(blocks)], axis=1)
        rows_out[pl.ds(p, 1), :] = high * CHUNK + low
        return carry

    loop(dom, rows, 0)

    def high(p):
        return rows_out[pl.ds(p, 1), :] >> SHIFT

    def low(p):
        return rows_out[pl.ds(p, 1), :] & (CHUNK - 1)

    total = add_mirrors(dom, received, high, low, feats, blocks, masters)
    divide(total, own, degree, mean)
    folded = jnp.concatenate([mean[:, a * CHUNK : (a + 1) * CHUNK] for a in range(parts)], axis=0)

    def one(p, carry):
        found = dot(folded, one_hot(low(p), CHUNK))
        chosen = jnp.zeros((feats, capacity), F32)
        for a in range(parts):
            chosen = chosen + keep(high(p) == a, found[a * feats : (a + 1) * feats])
        asked[p] = chosen.astype(BF16)
        return carry

    loop(dom, one, 0)
    out[:feats] = features[...]
    out[feats:] = mean[...]


def first_mean(dom, received, features, own, degree, capacity):
    feats, masters = own.shape
    return call(
        first_mean_body,
        (
            jax.ShapeDtypeStruct((2 * feats, masters), BF16),
            jax.ShapeDtypeStruct((dom, feats, capacity), BF16),
            jax.ShapeDtypeStruct((dom, capacity), I32),
        ),
        (received, features, own, degree),
        scratch=(pltpu.VMEM((feats, masters), BF16),),
        flops=2 * received.size * masters,
        moved=received.size * 2,
    )


def collect_body(order, received, reps, out):
    feats = out.shape[0]
    for n in range(0, reps.shape[1], CHUNK):
        at = slice(n, n + CHUNK)
        spots = one_hot(reps[1:2, at], received.shape[2])
        out[:, at] = pick_all(order, received, spots, reps[0:1, at], feats).astype(BF16)


def bring_body(masks_hbm, masks, arrived):
    for copy in fetch(masks_hbm, masks, arrived):
        copy.wait()


def weights_body(feat, me, self_one, neigh_one, self_two, neigh_two, both_out, both_own, mirror_own, self_own, neigh_own):
    rows_one = self_one.shape[0] // feat
    rows_two = neigh_two.shape[0] // feat
    wide_one = self_one.shape[1] // feat
    wide_two = neigh_two.shape[1] // feat

    def turned(pieces):
        return jnp.concatenate([piece.astype(F32) for piece in pieces], axis=0).T.astype(BF16)

    def fill(f):
        def block(weight, rows, k):
            return weight[(f ^ k) * rows : ((f ^ k) + 1) * rows, :]

        def own(values, wide):
            return values[f * wide : (f + 1) * wide]

        ones = [[block(w, rows_one, k) for w in (self_one, neigh_one)] for k in range(feat)]
        both = turned([piece for pair in ones for piece in pair])
        both_out[...] = both
        both_own[...] = own(both, wide_one)
        mirror_own[...] = own(turned([pair[i] for i in range(2) for pair in ones]), wide_one)
        self_own[...] = own(turned([self_two[...]]), wide_two)
        neigh_own[...] = own(turned([block(neigh_two, rows_two, k) for k in range(feat)]), wide_two)

    for f in range(feat):
        pl.when(me[0] == f)(functools.partial(fill, f))


def turn_weights(feat, me, self_one, neigh_one, self_two, neigh_two):
    wide_one = self_one.shape[1] // feat
    wide_two = neigh_two.shape[1] // feat
    depth = 2 * self_one.shape[0]
    shapes = [
        (self_one.shape[1], depth),
        (wide_one, depth),
        (wide_one, depth),
        (wide_two, self_two.shape[0]),
        (wide_two, neigh_two.shape[0]),
    ]
    return call(
        functools.partial(weights_body, feat),
        tuple(jax.ShapeDtypeStruct(shape, BF16) for shape in shapes),
        (me.reshape(1), self_one, neigh_one, self_two, neigh_two),
        smem=(0,),
        moved=2 * sum(a * b for a, b in shapes),
    )


def stack(refs, at=slice(None)):
    return jnp.concatenate([ref[:, at] for ref in refs], axis=0)


def hidden_body(feat, both_t, both_own, self_two_own, *refs):
    own_out, self_out = refs[feat:]
    values = stack(refs[:feat])
    own_out[...] = jnp.maximum(dot(both_own[...], values), 0.0).astype(BF16)
    hidden = jnp.maximum(dot(both_t[...], values), 0.0).astype(BF16)
    self_out[...] = dot(self_two_own[...], hidden)


def second_body(feat, order, cols, mirror_own, own, masks, reps, *refs):
    rows = refs[: 2 * feat]
    own_out, out, local, mirror = refs[2 * feat :]
    feats, masters = own.shape
    head = masters // LANES
    for i in range(head):
        local[i] = own[:, i * LANES : (i + 1) * LANES]
    for n in range(0, reps.shape[1], CHUNK):
        result = dot(mirror_own[...], stack(rows, slice(n, n + CHUNK)))
        values = jnp.maximum(result, 0.0).astype(BF16)
        for i in range(CHUNK // LANES):
            local[head + n // LANES + i] = values[:, i * LANES : (i + 1) * LANES]
    aggregate(cols, local, masks, head, own_out, mirror)
    send(order, mirror, reps, out, False)


def second_sums(order, cols, inputs, means, mirror_own, own, masks, reps, capacity):
    feats, masters = own.shape
    mirrors = reps.shape[1]
    rows = capacity // LANES * feats
    return call(
        functools.partial(second_body, len(means), order),
        (
            jax.ShapeDtypeStruct((feats, masters), F32),
            jax.ShapeDtypeStruct((len(order), rows, LANES), BF16),
        ),
        (cols, mirror_own, own, masks, reps) + inputs + means,
        smem=(0,),
        scratch=(
            pltpu.VMEM((masks.shape[0], feats, LANES), BF16),
            pltpu.VMEM((feats, mirrors), BF16),
        ),
        flops=2 * feats * masks.size,
        moved=masks.size,
    )


def second_mean_body(received, rows, own, degree, out):
    feats, masters = own.shape
    dom, capacity = rows.shape

    def high(p):
        return rows[pl.ds(p, 1), :] >> SHIFT

    def low(p):
        return rows[pl.ds(p, 1), :] & (CHUNK - 1)

    total = add_mirrors(dom, received, high, low, feats, capacity // LANES, masters)
    divide(total, own, degree, out)


def embed_body(count, neigh_t, total, *refs):
    out = refs[count]
    out[...] = (total[...] + dot(neigh_t[...], stack(refs[:count]))).astype(out.dtype)


def embed(neigh_t, total, blocks, dtype):
    return call(
        functools.partial(embed_body, len(blocks)),
        jax.ShapeDtypeStruct(total.shape, dtype),
        (neigh_t, total) + blocks,
        flops=2 * total.size * neigh_t.shape[1],
        moved=10 * total.size,
    )


def on_device(
    features, tile_mask, tile_cols, replicas, degree, self_one, neigh_one, self_two, neigh_two
):
    dom = lax.axis_size("dom")
    feat = lax.axis_size("feat")
    feats, masters = features.shape
    mirrors = replicas.shape[1]
    hidden_feats = self_one.shape[1] // feat
    capacity = -(-(2 * mirrors // dom) // LANES) * LANES
    cols = tile_cols.T
    degree = degree.reshape(1, masters)

    order = ORDER if dom == len(ORDER) else tuple(range(dom))

    def exchange(blocks):
        return lax.all_to_all(
            blocks, "dom", split_axis=0, concat_axis=0, tiled=True, axis_index_groups=[list(order)]
        )

    me = lax.axis_index("feat")

    def swap(values, k):
        return lax.ppermute(values, "feat", [(i, i ^ k) for i in range(feat)])

    def gather(blocks, stop=feat):
        blocks = list(blocks)
        for k in range(len(blocks), stop):
            low = k & -k
            blocks.append(swap(blocks[k ^ low], low))
        return tuple(blocks)

    last = feat - 1
    together = lax.optimization_barrier

    def spread(columns):
        if dom != GROUP:
            return (exchange(jnp.broadcast_to(columns[None], (dom,) + columns.shape)),)
        half = dom // 2
        others = list(range(1, half))

        def swap(values, k):
            return lax.ppermute(values, "dom", [(i, i ^ k) for i in range(dom)])

        far = swap(columns, half)
        near = [swap(columns, k) for k in others]
        return (*near, far, *[swap(far, k) for k in others])

    received = spread(features)
    masks = transpose_masks(tile_mask)
    own_one, mirror_in, outgoing, kept_masks = first_sums(
        order, cols, received, features, masks, replicas, capacity
    )
    sums = exchange(outgoing)
    own_both, asked, rows = first_mean(dom, sums, features, own_one, degree, capacity)
    own_both, weights = together((own_both, (self_one, neigh_one, self_two, neigh_two)))
    slots = exchange(asked)
    inputs = gather((own_both,))
    both_t, both_own, mirror_own, self_two_own, neigh_two_own = turn_weights(feat, me, *weights)
    slots, both_t, both_own, mirror_own, self_two_own, neigh_two_own = together(
        (slots, both_t, both_own, mirror_own, self_two_own, neigh_two_own)
    )
    mirror_mean = call(
        functools.partial(collect_body, order),
        jax.ShapeDtypeStruct((feats, mirrors), BF16),
        (slots, replicas),
        flops=2 * slots.size * mirrors,
        moved=2 * slots.size,
    )
    mirror_mean, kept_masks = together((mirror_mean, kept_masks))
    means = gather((mirror_mean,), last)
    near_masks = call(
        bring_body,
        jax.ShapeDtypeStruct(masks.shape, MASK),
        (kept_masks,),
        hbm=(0,),
        limit=44,
        scratch=(pltpu.SemaphoreType.DMA((PIECES,)),),
        moved=2 * masks.size,
    )
    hidden, self_part = call(
        functools.partial(hidden_body, feat),
        (
            jax.ShapeDtypeStruct((hidden_feats, masters), BF16),
            jax.ShapeDtypeStruct((self_two_own.shape[0], masters), F32),
        ),
        (both_t, both_own, self_two_own) + inputs,
        flops=2 * masters * (4 * self_one.size + self_two_own.size),
        moved=masters * 1024,
    )
    means, near_masks, hidden, self_part, neigh_two_own = together(
        (means, near_masks, hidden, self_part, neigh_two_own)
    )
    own_two, outgoing = second_sums(
        order, cols, gather((mirror_in,)), gather(means), mirror_own, hidden, near_masks, replicas, capacity
    )
    mean_two = call(
        second_mean_body,
        jax.ShapeDtypeStruct((hidden_feats, masters), BF16),
        (exchange(outgoing), rows, own_two, degree),
        flops=2 * hidden_feats * dom * capacity * masters,
        moved=2 * hidden_feats * dom * capacity,
    )
    blocks = gather((mean_two,))
    total = self_part
    for start, stop in ((0, 2), (2, 3), (3, 4)):
        weights = neigh_two_own[:, start * hidden_feats : stop * hidden_feats]
        total = embed(weights, total, blocks[start:stop], BF16 if stop == feat else F32)
    return total


def solution(mesh):
    return jax.shard_map(
        on_device,
        mesh=mesh,
        in_specs=(
            P("feat", "dom"),
            P("dom", None, None, None),
            P("dom", None),
            P(None, "dom"),
            P("dom"),
            P(),
            P(),
            P(),
            P(),
        ),
        out_specs=P("feat", "dom"),
        check_vma=False,
    )
```

```python
import functools

import jax
import jax.numpy as jnp
from jax import lax
from jax.experimental import pallas as pl
from jax.experimental.pallas import tpu as pltpu
from jax.sharding import PartitionSpec as P

F32 = jnp.float32
BF16 = jnp.bfloat16
I32 = jnp.int32
MASK = jnp.float8_e4m3fn
LANES = 128
SHIFT = 8
CHUNK = 1 << SHIFT
GROUP = 8
ORDER = (5, 2, 3, 7, 1, 0, 4, 6)
INDEX_ROWS = 16
VMEM = pl.BlockSpec(memory_space=pltpu.VMEM)
SMEM = pl.BlockSpec(memory_space=pltpu.SMEM)
HBM = pl.BlockSpec(memory_space=pltpu.HBM)
MASK_PIECES = 8


def call(body, out_shape, operands, smem=(), hbm=(), hbm_out=(), scratch=(), flops=0, moved=0, limit=20):
    def place(i):
        return SMEM if i in smem else HBM if i in hbm else VMEM

    return pl.pallas_call(
        body,
        out_shape=out_shape,
        in_specs=[place(i) for i in range(len(operands))],
        out_specs=(
            tuple(HBM if i in hbm_out else VMEM for i in range(len(out_shape)))
            if isinstance(out_shape, tuple)
            else VMEM
        ),
        scratch_shapes=list(scratch),
        compiler_params=pltpu.CompilerParams(vmem_limit_bytes=limit << 20),
        cost_estimate=pl.CostEstimate(flops=flops, bytes_accessed=moved, transcendentals=0),
    )(*operands)


def dot(left, right, dims=(1, 0)):
    return lax.dot_general(
        left, right, (((dims[0],), (dims[1],)), ((), ())), preferred_element_type=F32
    )


def one_hot(index_row, depth):
    side = min(depth, CHUNK)
    n = index_row.shape[1]
    rows = lax.broadcasted_iota(I32, (side, n), 0).astype(F32).astype(BF16)
    blocks = []
    for start in range(0, depth, side):
        here = (index_row >= start) & (index_row < start + side)
        spot = jnp.where(here, index_row - start, -1).astype(F32).astype(BF16)
        blocks.append(jnp.where(rows == spot, jnp.ones_like(rows), jnp.zeros_like(rows)))
    return blocks[0] if len(blocks) == 1 else jnp.concatenate(blocks, axis=0)


def keep(condition, values):
    return jnp.where(condition, values, jnp.zeros_like(values))


def loop(count, body, carry):
    if count <= GROUP:
        for i in range(count):
            carry = body(i, carry)
        return carry
    return lax.fori_loop(0, count, body, carry)


def masks_body(tile_mask, out, blocks, arrived):
    tiles, stored, side, _ = blocks.shape
    copies = transfer(tile_mask, blocks, tiles, arrived)
    step = tiles // len(copies)
    for i in range(tiles):
        if i % step == 0:
            copies[i // step].wait()
        for k in range(stored):
            block = blocks[i, k].astype(F32).astype(BF16)
            out[i, k * side : (k + 1) * side, :] = block.T


def transpose_masks(tile_mask):
    tiles, stored, side, _ = tile_mask.shape
    return call(
        masks_body,
        jax.ShapeDtypeStruct((tiles, stored * side, side), BF16),
        (tile_mask,),
        hbm=(0,),
        limit=47,
        scratch=(
            pltpu.VMEM(tile_mask.shape, I32),
            pltpu.SemaphoreType.DMA((MASK_PIECES,)),
        ),
        moved=6 * tile_mask.size,
    )


def index_rows(part, slot, row, names, blocks):
    lane_shift = LANES.bit_length() - 1
    shape = (len(names) * INDEX_ROWS, part.shape[1])
    at = lax.broadcasted_iota(I32, (shape[0], 1), 0)
    place = at % INDEX_ROWS
    name = jnp.zeros_like(at)
    for k, q in enumerate(names):
        name = jnp.where(at // INDEX_ROWS == k, q, name)
    wanted = jnp.where(place < 2 * blocks, name * blocks + place % blocks, -1)
    here = jnp.broadcast_to(wanted, shape) == part * blocks + (slot >> lane_shift)
    digits = jnp.where(
        jnp.broadcast_to(place < blocks, shape),
        jnp.broadcast_to((row >> SHIFT).astype(F32), shape),
        jnp.broadcast_to((row & (CHUNK - 1)).astype(F32), shape),
    )
    return dot(keep(here, digits).astype(BF16), one_hot(slot & (LANES - 1), LANES), (1, 1)).astype(BF16)


def pick(blocks, names, spots, part, feats):
    found = dot(jnp.concatenate(blocks, axis=0), spots)
    total = jnp.zeros((feats, spots.shape[1]), F32)
    for k, name in enumerate(names):
        total = total + keep(part == name, found[k * feats : (k + 1) * feats])
    return total


def pick_all(order, received, spots, part, feats):
    dom = received.shape[0]
    if dom == GROUP:
        return pick([received[k] for k in range(dom)], order, spots, part, feats)

    def add_group(g, total):
        blocks = [received[g * GROUP + k] for k in range(GROUP)]
        return total + pick(blocks, range(GROUP), spots, part - g * GROUP, feats)

    return lax.fori_loop(0, dom // GROUP, add_group, jnp.zeros((feats, spots.shape[1]), F32))


def transfer(source, target, rows, done):
    step = rows // done.shape[0]
    copies = []
    for i in range(done.shape[0]):
        at = pl.ds(i * step, step)
        copies.append(pltpu.make_async_copy(source.at[at], target.at[at], done.at[i]))
        copies[-1].start()
    return copies


def aggregate(cols, local, masks, head, own_out, mirror, narrow=None):
    stored = masks.shape[1] // LANES
    for i in range(masks.shape[0]):
        chosen = jnp.concatenate([local[cols[k, i]] for k in range(stored)], axis=1)
        row = masks[i]
        if narrow is not None:
            narrow[i] = row.astype(MASK)
        summed = dot(chosen, row.astype(BF16))
        if i < head:
            own_out[:, i * LANES : (i + 1) * LANES] = summed
        else:
            at = (i - head) * LANES
            mirror[:, at : at + LANES] = summed.astype(BF16)


def send(order, mirror, reps, out, with_index):
    feats = mirror.shape[0]
    dom = out.shape[0]
    rows = out.shape[1] // feats * feats
    blocks = rows // feats
    part, slot, row = reps[0:1, :], reps[1:2, :], reps[2:3, :]
    slot_places = one_hot(slot, blocks * LANES)
    values = mirror[...]

    def group(first, names, part):
        spread = jnp.concatenate([keep(part == name, values) for name in names], axis=0)
        placed = dot(spread, slot_places, (1, 1)).astype(BF16)
        for k in range(GROUP):
            for b in range(blocks):
                block = placed[k * feats : (k + 1) * feats, b * LANES : (b + 1) * LANES]
                out[first + k, b * feats : (b + 1) * feats, :] = block
        if with_index:
            index = index_rows(part, slot, row, names, blocks)
            for k in range(GROUP):
                out[first + k, rows:, :] = index[k * INDEX_ROWS : (k + 1) * INDEX_ROWS]

    if dom == GROUP:
        group(0, order, part)
    else:

        def one(g, carry):
            group(g * GROUP, range(GROUP), part - g * GROUP)
            return carry

        lax.fori_loop(0, dom // GROUP, one, 0)


def first_body(order, cols, own, masks, reps, *refs):
    received = refs[:-6]
    own_out, all_out, out, narrow, local, mirror = refs[-6:]
    feats, masters = own.shape
    head = masters // LANES
    for i in range(head):
        local[i] = own[:, i * LANES : (i + 1) * LANES]
    for n in range(0, reps.shape[1], CHUNK):
        at = slice(n, n + CHUNK)
        spots = one_hot(reps[2:3, at], masters)
        part = reps[0:1, at]
        if len(received) == 1:
            values = pick_all(order, received[0], spots, part, feats)
        else:
            part = part ^ lax.axis_index("dom")
            blocks = [ref[...] for ref in received]
            values = pick(blocks, range(1, len(blocks) + 1), spots, part, feats)
        values = values.astype(BF16)
        all_out[:, at] = values
        for i in range(CHUNK // LANES):
            local[head + n // LANES + i] = values[:, i * LANES : (i + 1) * LANES]
    aggregate(cols, local, masks, head, own_out, mirror, narrow)
    send(order, mirror, reps, out, True)


def first_sums(order, cols, received, own, masks, reps, capacity):
    feats, masters = own.shape
    mirrors = reps.shape[1]
    rows = capacity // LANES * feats + INDEX_ROWS
    tiles = masks.shape[0]
    return call(
        functools.partial(first_body, order),
        (
            jax.ShapeDtypeStruct((feats, masters), F32),
            jax.ShapeDtypeStruct((feats, mirrors), BF16),
            jax.ShapeDtypeStruct((len(order), rows, LANES), BF16),
            jax.ShapeDtypeStruct(masks.shape, MASK),
        ),
        (cols, own, masks, reps) + received,
        smem=(0,),
        scratch=(
            pltpu.VMEM((tiles, feats, LANES), BF16),
            pltpu.VMEM((feats, mirrors), BF16),
        ),
        flops=2 * feats * masks.size,
        moved=2 * masks.size,
    )


def message(received, p, feats, blocks):
    return jnp.concatenate([received[p, b * feats : (b + 1) * feats, :] for b in range(blocks)], axis=1)


def add_mirrors(dom, received, high, low, feats, blocks, masters):
    parts = masters // CHUNK

    def add(p, total):
        values = message(received, p, feats, blocks)
        spread = jnp.concatenate([keep(high(p) == a, values) for a in range(parts)], axis=0)
        return total + dot(spread, one_hot(low(p), CHUNK), (1, 1))

    return loop(dom, add, jnp.zeros((parts * feats, CHUNK), F32))


def divide(total, own, degree, out):
    feats, masters = own.shape
    for a in range(masters // CHUNK):
        at = slice(a * CHUNK, (a + 1) * CHUNK)
        whole = own[:, at] + total[a * feats : (a + 1) * feats]
        out[:, at] = (whole / degree[:, at].astype(F32)).astype(BF16)


def first_mean_body(received, features, mirror_in, own, degree, out, asked_hbm, rows_out, mean, asked, left):
    feats, masters = own.shape
    dom, capacity = rows_out.shape
    blocks = capacity // LANES
    parts = masters // CHUNK

    def rows(p, carry):
        coded = received[p, blocks * feats :, :].astype(F32).astype(I32)
        high = jnp.concatenate([coded[b : b + 1] for b in range(blocks)], axis=1)
        low = jnp.concatenate([coded[blocks + b : blocks + b + 1] for b in range(blocks)], axis=1)
        rows_out[pl.ds(p, 1), :] = high * CHUNK + low
        return carry

    loop(dom, rows, 0)

    def high(p):
        return rows_out[pl.ds(p, 1), :] >> SHIFT

    def low(p):
        return rows_out[pl.ds(p, 1), :] & (CHUNK - 1)

    total = add_mirrors(dom, received, high, low, feats, blocks, masters)
    divide(total, own, degree, mean)
    folded = jnp.concatenate([mean[:, a * CHUNK : (a + 1) * CHUNK] for a in range(parts)], axis=0)

    def serve(p, carry):
        found = dot(folded, one_hot(low(p), CHUNK))
        chosen = jnp.zeros((feats, capacity), F32)
        for a in range(parts):
            chosen = chosen + keep(high(p) == a, found[a * feats : (a + 1) * feats])
        asked[p] = chosen.astype(BF16)
        return carry

    def one(p, carry):
        serve(p, carry)
        copies[p].start()
        return carry

    if dom == GROUP:
        copies = [pltpu.make_async_copy(asked.at[p], asked_hbm.at[p], left.at[p]) for p in range(dom)]
        loop(dom, one, 0)
    else:
        copies = [pltpu.make_async_copy(asked, asked_hbm, left.at[0])]
        lax.fori_loop(0, dom, serve, 0)
        copies[0].start()
    out[:feats] = features[...]
    out[feats : 2 * feats] = mean[...]
    for n in range(mirror_in.shape[1] // masters):
        out[(2 + n) * feats : (3 + n) * feats] = mirror_in[:, n * masters : (n + 1) * masters]
    for copy in copies:
        copy.wait()


def first_mean(dom, received, features, mirror_in, own, degree, capacity):
    feats, masters = own.shape
    rows = (2 + mirror_in.shape[1] // masters) * feats
    return call(
        first_mean_body,
        (
            jax.ShapeDtypeStruct((rows, masters), BF16),
            jax.ShapeDtypeStruct((dom, feats, capacity), BF16),
            jax.ShapeDtypeStruct((dom, capacity), I32),
        ),
        (received, features, mirror_in, own, degree),
        hbm_out=(1,),
        scratch=(
            pltpu.VMEM((feats, masters), BF16),
            pltpu.VMEM((dom, feats, capacity), BF16),
            pltpu.SemaphoreType.DMA((dom if dom == GROUP else 1,)),
        ),
        flops=2 * received.size * masters,
        moved=received.size * 2,
    )


def collect_body(order, received, reps, out):
    feats = out.shape[0]
    for n in range(0, reps.shape[1], CHUNK):
        at = slice(n, n + CHUNK)
        spots = one_hot(reps[1:2, at], received.shape[2])
        out[:, at] = pick_all(order, received, spots, reps[0:1, at], feats).astype(BF16)


def weights_body(feat, me, self_one, neigh_one, self_two, neigh_two, out):
    rows_one = self_one.shape[0] // feat
    rows_two = neigh_two.shape[0] // feat
    hidden = self_one.shape[1]
    wide = hidden // feat

    def turned(pieces):
        return jnp.concatenate([piece.astype(F32) for piece in pieces], axis=0).T.astype(BF16)

    def fill(f):
        def block(weight, rows, k):
            return weight[(f ^ k) * rows : ((f ^ k) + 1) * rows, :]

        def own(values):
            return values[f * wide : (f + 1) * wide]

        ones = [[block(w, rows_one, k) for w in (self_one, neigh_one)] for k in range(feat)]
        both = turned([piece for pair in ones for piece in pair])
        parts = [
            both,
            own(both),
            own(turned([pair[i] for i in range(2) for pair in ones])),
            own(turned([self_two[...]])),
            own(turned([block(neigh_two, rows_two, k) for k in range(feat)])),
        ]
        out[...] = jnp.concatenate(parts, axis=0)

    for f in range(feat):
        pl.when(me[0] == f)(functools.partial(fill, f))


def turn_weights(feat, me, self_one, neigh_one, self_two, neigh_two):
    hidden = self_one.shape[1]
    shape = (hidden + 4 * (hidden // feat), 2 * self_one.shape[0])
    return call(
        functools.partial(weights_body, feat),
        jax.ShapeDtypeStruct(shape, BF16),
        (me.reshape(1), self_one, neigh_one, self_two, neigh_two),
        smem=(0,),
        moved=2 * shape[0] * shape[1],
    )


def stack(refs, at=slice(None)):
    return jnp.concatenate([ref[:, at] for ref in refs], axis=0)


def hidden_body(feat, weights, *refs):
    own_out, self_out, mirror_own, neigh_own = refs[feat:]
    wide = own_out.shape[0]
    whole = feat * wide
    depth = weights.shape[1] // feat
    values = jnp.concatenate([ref[:depth] for ref in refs[:feat]], axis=0)
    own_out[...] = jnp.maximum(dot(weights[whole : whole + wide], values), 0.0).astype(BF16)
    hidden = jnp.maximum(dot(weights[:whole], values), 0.0).astype(BF16)
    self_out[...] = dot(weights[whole + 2 * wide : whole + 3 * wide], hidden)
    mirror_own[...] = weights[whole + wide : whole + 2 * wide]
    neigh_own[...] = weights[whole + 3 * wide : whole + 4 * wide]


def second_body(feat, order, cols, mirror_own, own, masks, reps, *refs):
    packs, means = refs[:feat], refs[feat : 2 * feat]
    own_out, out, local, mirror = refs[2 * feat :]
    feats, masters = own.shape
    head = masters // LANES
    for i in range(head):
        local[i] = own[:, i * LANES : (i + 1) * LANES]
    for n in range(0, reps.shape[1], CHUNK):
        block, start = n // masters, n % masters
        depth = means[0].shape[0]
        rows = [ref[(2 + block) * depth : (3 + block) * depth, start : start + CHUNK] for ref in packs]
        rows += [ref[:, n : n + CHUNK] for ref in means]
        result = dot(mirror_own[...], jnp.concatenate(rows, axis=0))
        values = jnp.maximum(result, 0.0).astype(BF16)
        for i in range(CHUNK // LANES):
            local[head + n // LANES + i] = values[:, i * LANES : (i + 1) * LANES]
    aggregate(cols, local, masks, head, own_out, mirror)
    send(order, mirror, reps, out, False)


def second_sums(order, cols, inputs, means, mirror_own, own, masks, reps, capacity):
    feats, masters = own.shape
    mirrors = reps.shape[1]
    rows = capacity // LANES * feats
    return call(
        functools.partial(second_body, len(means), order),
        (
            jax.ShapeDtypeStruct((feats, masters), F32),
            jax.ShapeDtypeStruct((len(order), rows, LANES), BF16),
        ),
        (cols, mirror_own, own, masks, reps) + inputs + means,
        smem=(0,),
        scratch=(
            pltpu.VMEM((masks.shape[0], feats, LANES), BF16),
            pltpu.VMEM((feats, mirrors), BF16),
        ),
        flops=2 * feats * masks.size,
        moved=masks.size,
    )


def second_mean_body(received, rows, own, degree, out):
    feats, masters = own.shape
    dom, capacity = rows.shape

    def high(p):
        return rows[pl.ds(p, 1), :] >> SHIFT

    def low(p):
        return rows[pl.ds(p, 1), :] & (CHUNK - 1)

    total = add_mirrors(dom, received, high, low, feats, capacity // LANES, masters)
    divide(total, own, degree, out)


def embed_body(count, neigh_t, total, *refs):
    out = refs[count]
    out[...] = (total[...] + dot(neigh_t[...], stack(refs[:count]))).astype(out.dtype)


def embed(neigh_t, total, blocks, dtype):
    return call(
        functools.partial(embed_body, len(blocks)),
        jax.ShapeDtypeStruct(total.shape, dtype),
        (neigh_t, total) + blocks,
        flops=2 * total.size * neigh_t.shape[1],
        moved=10 * total.size,
    )


def on_device(
    features, tile_mask, tile_cols, replicas, degree, self_one, neigh_one, self_two, neigh_two
):
    dom = lax.axis_size("dom")
    feat = lax.axis_size("feat")
    feats, masters = features.shape
    mirrors = replicas.shape[1]
    hidden_feats = self_one.shape[1] // feat
    capacity = -(-(2 * mirrors // dom) // LANES) * LANES
    cols = tile_cols.T
    degree = degree.reshape(1, masters)

    order = ORDER if dom == len(ORDER) else tuple(range(dom))

    def exchange(blocks):
        return lax.all_to_all(
            blocks, "dom", split_axis=0, concat_axis=0, tiled=True, axis_index_groups=[list(order)]
        )

    me = lax.axis_index("feat")

    def swap(values, k):
        return lax.ppermute(values, "feat", [(i, i ^ k) for i in range(feat)])

    def gather(blocks, stop=feat):
        blocks = list(blocks)
        for k in range(len(blocks), stop):
            low = k & -k
            blocks.append(swap(blocks[k ^ low], low))
        return tuple(blocks)

    last = feat - 1
    together = lax.optimization_barrier

    def spread(columns):
        if dom != GROUP:
            return (exchange(jnp.broadcast_to(columns[None], (dom,) + columns.shape)),)
        half = dom // 2
        others = list(range(1, half))

        def swap(values, k):
            return lax.ppermute(values, "dom", [(i, i ^ k) for i in range(dom)])

        far = swap(columns, half)
        near = [swap(columns, k) for k in others]
        return (*near, far, *[swap(far, k) for k in others])

    received = spread(features)
    masks = transpose_masks(tile_mask)
    own_one, mirror_in, outgoing, narrow = first_sums(
        order, cols, received, features, masks, replicas, capacity
    )
    sums = exchange(outgoing)
    pack, asked, rows = first_mean(dom, sums, features, mirror_in, own_one, degree, capacity)
    pack, weights = together((pack, (self_one, neigh_one, self_two, neigh_two)))
    slots = exchange(asked)
    across = swap(pack, 2)
    weights = turn_weights(feat, me, *weights)
    slots, weights = together((slots, weights))
    mirror_mean = call(
        functools.partial(collect_body, order),
        jax.ShapeDtypeStruct((feats, mirrors), BF16),
        (slots, replicas),
        flops=2 * slots.size * mirrors,
        moved=2 * slots.size,
    )
    means = gather((mirror_mean,), last)
    mirror_mean, pack, across = together((mirror_mean, pack, across))
    packs = (pack, swap(pack, 1), across, swap(across, 1))
    hidden, self_part, mirror_own, neigh_two_own = call(
        functools.partial(hidden_body, feat),
        (
            jax.ShapeDtypeStruct((hidden_feats, masters), BF16),
            jax.ShapeDtypeStruct((hidden_feats, masters), F32),
            jax.ShapeDtypeStruct((hidden_feats, weights.shape[1]), BF16),
            jax.ShapeDtypeStruct((hidden_feats, weights.shape[1]), BF16),
        ),
        (weights,) + packs,
        flops=2 * masters * weights.size,
        moved=masters * 1024,
    )
    means, hidden, self_part, mirror_own, neigh_two_own = together(
        (means, hidden, self_part, mirror_own, neigh_two_own)
    )
    own_two, outgoing = second_sums(
        order, cols, packs, gather(means), mirror_own, hidden, narrow, replicas, capacity
    )
    mean_two = call(
        second_mean_body,
        jax.ShapeDtypeStruct((hidden_feats, masters), BF16),
        (exchange(outgoing), rows, own_two, degree),
        flops=2 * hidden_feats * dom * capacity * masters,
        moved=2 * hidden_feats * dom * capacity,
    )
    blocks = gather((mean_two,))
    total = self_part
    for start, stop in ((0, 3), (3, 4)):
        weights = neigh_two_own[:, start * hidden_feats : stop * hidden_feats]
        total = embed(weights, total, blocks[start:stop], BF16 if stop == feat else F32)
    return total


def solution(mesh):
    return jax.shard_map(
        on_device,
        mesh=mesh,
        in_specs=(
            P("feat", "dom"),
            P("dom", None, None, None),
            P("dom", None),
            P(None, "dom"),
            P("dom"),
            P(),
            P(),
            P(),
            P(),
        ),
        out_specs=P("feat", "dom"),
        check_vma=False,
    )
```

```python
import functools

import jax
import jax.numpy as jnp
from jax import lax
from jax.experimental import pallas as pl
from jax.experimental.pallas import tpu as pltpu
from jax.sharding import PartitionSpec as P

F32 = jnp.float32
BF16 = jnp.bfloat16
I32 = jnp.int32
MASK = jnp.float8_e4m3fn
LANES = 128
SHIFT = 8
CHUNK = 1 << SHIFT
GROUP = 8
ORDER = (5, 2, 3, 7, 1, 0, 4, 6)
INDEX_ROWS = 16
VMEM = pl.BlockSpec(memory_space=pltpu.VMEM)
SMEM = pl.BlockSpec(memory_space=pltpu.SMEM)
HBM = pl.BlockSpec(memory_space=pltpu.HBM)
PIECES = 4
MASK_PIECES = 8
SPARE = 10


def call(body, out_shape, operands, smem=(), hbm=(), hbm_out=(), scratch=(), flops=0, moved=0, limit=20):
    def place(i):
        return SMEM if i in smem else HBM if i in hbm else VMEM

    return pl.pallas_call(
        body,
        out_shape=out_shape,
        in_specs=[place(i) for i in range(len(operands))],
        out_specs=(
            tuple(HBM if i in hbm_out else VMEM for i in range(len(out_shape)))
            if isinstance(out_shape, tuple)
            else VMEM
        ),
        scratch_shapes=list(scratch),
        compiler_params=pltpu.CompilerParams(vmem_limit_bytes=limit << 20),
        cost_estimate=pl.CostEstimate(flops=flops, bytes_accessed=moved, transcendentals=0),
    )(*operands)


def dot(left, right, dims=(1, 0)):
    return lax.dot_general(
        left, right, (((dims[0],), (dims[1],)), ((), ())), preferred_element_type=F32
    )


def one_hot(index_row, depth):
    side = min(depth, CHUNK)
    n = index_row.shape[1]
    rows = lax.broadcasted_iota(I32, (side, n), 0).astype(F32).astype(BF16)
    blocks = []
    for start in range(0, depth, side):
        here = (index_row >= start) & (index_row < start + side)
        spot = jnp.where(here, index_row - start, -1).astype(F32).astype(BF16)
        blocks.append(jnp.where(rows == spot, jnp.ones_like(rows), jnp.zeros_like(rows)))
    return blocks[0] if len(blocks) == 1 else jnp.concatenate(blocks, axis=0)


def keep(condition, values):
    return jnp.where(condition, values, jnp.zeros_like(values))


def loop(count, body, carry):
    if count <= GROUP:
        for i in range(count):
            carry = body(i, carry)
        return carry
    return lax.fori_loop(0, count, body, carry)


def masks_body(tile_mask, out, blocks, arrived):
    tiles, stored, side, _ = blocks.shape
    copies = fetch(tile_mask, blocks, arrived)
    step = tiles // len(copies)
    for i in range(tiles):
        if i % step == 0:
            copies[i // step].wait()
        for k in range(stored):
            block = blocks[i, k].astype(F32).astype(BF16)
            out[i, k * side : (k + 1) * side, :] = block.T


def transpose_masks(tile_mask):
    tiles, stored, side, _ = tile_mask.shape
    return call(
        masks_body,
        jax.ShapeDtypeStruct((tiles, stored * side, side), BF16),
        (tile_mask,),
        hbm=(0,),
        limit=47,
        scratch=(
            pltpu.VMEM(tile_mask.shape, I32),
            pltpu.SemaphoreType.DMA((MASK_PIECES,)),
        ),
        moved=6 * tile_mask.size,
    )


def index_rows(part, row, slot_places, names):
    blocks = slot_places.shape[0] // LANES
    name = lax.broadcasted_iota(I32, (len(names), 1), 0)
    for k, q in enumerate(names):
        name = jnp.where(lax.broadcasted_iota(I32, (len(names), 1), 0) == k, q, name)
    mine = jnp.broadcast_to(name, (len(names), part.shape[1])) == part
    digits = [keep(mine, jnp.broadcast_to(d, mine.shape)) for d in (row >> SHIFT, row & (CHUNK - 1))]
    digits = jnp.concatenate(digits, axis=0).astype(F32).astype(BF16)
    found = dot(digits, slot_places, (1, 1))
    out = []
    for k in range(len(names)):
        pieces = [
            found[at : at + 1, b * LANES : (b + 1) * LANES]
            for at in (k, len(names) + k)
            for b in range(blocks)
        ]
        pieces.append(jnp.zeros((INDEX_ROWS - len(pieces), LANES), F32))
        out.append(jnp.concatenate(pieces, axis=0).astype(BF16))
    return out


def pick(blocks, names, spots, part, feats):
    found = dot(jnp.concatenate(blocks, axis=0), spots)
    total = jnp.zeros((feats, spots.shape[1]), F32)
    for k, name in enumerate(names):
        total = total + keep(part == name, found[k * feats : (k + 1) * feats])
    return total


def pick_all(order, received, spots, part, feats):
    dom = received.shape[0]
    if dom == GROUP:
        return pick([received[k] for k in range(dom)], order, spots, part, feats)

    def add_group(g, total):
        blocks = [received[g * GROUP + k] for k in range(GROUP)]
        return total + pick(blocks, range(GROUP), spots, part - g * GROUP, feats)

    return lax.fori_loop(0, dom // GROUP, add_group, jnp.zeros((feats, spots.shape[1]), F32))


def fetch(source, target, arrived):
    pieces = arrived.shape[0]
    step = target.shape[0] // pieces
    copies = []
    for i in range(pieces):
        at = pl.ds(i * step, step)
        copies.append(pltpu.make_async_copy(source.at[at], target.at[at], arrived.at[i]))
        copies[-1].start()
    return copies


def aggregate(cols, local, masks, head, own_out, mirror, narrow=None):
    stored = masks.shape[1] // LANES
    for i in range(masks.shape[0]):
        chosen = jnp.concatenate([local[cols[k, i]] for k in range(stored)], axis=1)
        row = masks[i]
        if narrow is not None:
            narrow[i] = row.astype(MASK)
        summed = dot(chosen, row.astype(BF16))
        if i < head:
            own_out[:, i * LANES : (i + 1) * LANES] = summed
        else:
            at = (i - head) * LANES
            mirror[:, at : at + LANES] = summed.astype(BF16)


def send(order, mirror, reps, out, with_index):
    feats = mirror.shape[0]
    dom = out.shape[0]
    rows = out.shape[1] // feats * feats
    blocks = rows // feats
    part, slot, row = reps[0:1, :], reps[1:2, :], reps[2:3, :]
    slot_places = one_hot(slot, blocks * LANES)
    values = mirror[...]

    def group(first, names, part):
        spread = jnp.concatenate([keep(part == name, values) for name in names], axis=0)
        placed = dot(spread, slot_places, (1, 1)).astype(BF16)
        for k in range(GROUP):
            for b in range(blocks):
                block = placed[k * feats : (k + 1) * feats, b * LANES : (b + 1) * LANES]
                out[first + k, b * feats : (b + 1) * feats, :] = block
        if with_index:
            for k, index in enumerate(index_rows(part, row, slot_places, names)):
                out[first + k, rows:, :] = index

    if dom == GROUP:
        group(0, order, part)
    else:

        def one(g, carry):
            group(g * GROUP, range(GROUP), part - g * GROUP)
            return carry

        lax.fori_loop(0, dom // GROUP, one, 0)


def first_body(order, cols, own, masks, reps, *refs):
    received = refs[:-8]
    own_out, all_out, out, kept, local, mirror, narrow, written = refs[-8:]
    feats, masters = own.shape
    head = masters // LANES
    for i in range(head):
        local[i] = own[:, i * LANES : (i + 1) * LANES]
    for n in range(0, reps.shape[1], CHUNK):
        at = slice(n, n + CHUNK)
        spots = one_hot(reps[2:3, at], masters)
        part = reps[0:1, at]
        if len(received) == 1:
            values = pick_all(order, received[0], spots, part, feats)
        else:
            part = part ^ lax.axis_index("dom")
            blocks = [ref[...] for ref in received]
            values = pick(blocks, range(1, len(blocks) + 1), spots, part, feats)
        values = values.astype(BF16)
        all_out[:, at] = values
        for i in range(CHUNK // LANES):
            local[head + n // LANES + i] = values[:, i * LANES : (i + 1) * LANES]
    aggregate(cols, local, masks, head, own_out, mirror, narrow)
    copy = pltpu.make_async_copy(narrow, kept.at[pl.ds(0, masks.shape[0])], written)
    copy.start()
    send(order, mirror, reps, out, True)
    copy.wait()


def first_sums(order, cols, received, own, masks, reps, capacity):
    feats, masters = own.shape
    mirrors = reps.shape[1]
    rows = capacity // LANES * feats + INDEX_ROWS
    tiles = masks.shape[0]
    return call(
        functools.partial(first_body, order),
        (
            jax.ShapeDtypeStruct((feats, masters), F32),
            jax.ShapeDtypeStruct((feats, mirrors), BF16),
            jax.ShapeDtypeStruct((len(order), rows, LANES), BF16),
            jax.ShapeDtypeStruct((SPARE * tiles,) + masks.shape[1:], MASK),
        ),
        (cols, own, masks, reps) + received,
        smem=(0,),
        hbm_out=(3,),
        limit=44,
        scratch=(
            pltpu.VMEM((tiles, feats, LANES), BF16),
            pltpu.VMEM((feats, mirrors), BF16),
            pltpu.VMEM(masks.shape, MASK),
            pltpu.SemaphoreType.DMA,
        ),
        flops=2 * feats * masks.size,
        moved=2 * masks.size,
    )


def message(received, p, feats, blocks):
    return jnp.concatenate([received[p, b * feats : (b + 1) * feats, :] for b in range(blocks)], axis=1)


def add_mirrors(dom, received, high, low, feats, blocks, masters):
    parts = masters // CHUNK

    def add(p, total):
        values = message(received, p, feats, blocks)
        spread = jnp.concatenate([keep(high(p) == a, values) for a in range(parts)], axis=0)
        return total + dot(spread, one_hot(low(p), CHUNK), (1, 1))

    return loop(dom, add, jnp.zeros((parts * feats, CHUNK), F32))


def divide(total, own, degree, out):
    feats, masters = own.shape
    for a in range(masters // CHUNK):
        at = slice(a * CHUNK, (a + 1) * CHUNK)
        whole = own[:, at] + total[a * feats : (a + 1) * feats]
        out[:, at] = (whole / degree[:, at].astype(F32)).astype(BF16)


def first_mean_body(received, features, own, degree, out, asked, rows_out, mean):
    feats, masters = own.shape
    dom, capacity = rows_out.shape
    blocks = capacity // LANES
    parts = masters // CHUNK

    def rows(p, carry):
        coded = received[p, blocks * feats :, :].astype(F32).astype(I32)
        high = jnp.concatenate([coded[b : b + 1] for b in range(blocks)], axis=1)
        low = jnp.concatenate([coded[blocks + b : blocks + b + 1] for b in range(blocks)], axis=1)
        rows_out[pl.ds(p, 1), :] = high * CHUNK + low
        return carry

    loop(dom, rows, 0)

    def high(p):
        return rows_out[pl.ds(p, 1), :] >> SHIFT

    def low(p):
        return rows_out[pl.ds(p, 1), :] & (CHUNK - 1)

    total = add_mirrors(dom, received, high, low, feats, blocks, masters)
    divide(total, own, degree, mean)
    folded = jnp.concatenate([mean[:, a * CHUNK : (a + 1) * CHUNK] for a in range(parts)], axis=0)

    def one(p, carry):
        found = dot(folded, one_hot(low(p), CHUNK))
        chosen = jnp.zeros((feats, capacity), F32)
        for a in range(parts):
            chosen = chosen + keep(high(p) == a, found[a * feats : (a + 1) * feats])
        asked[p] = chosen.astype(BF16)
        return carry

    loop(dom, one, 0)
    out[:feats] = features[...]
    out[feats:] = mean[...]


def first_mean(dom, received, features, own, degree, capacity):
    feats, masters = own.shape
    return call(
        first_mean_body,
        (
            jax.ShapeDtypeStruct((2 * feats, masters), BF16),
            jax.ShapeDtypeStruct((dom, feats, capacity), BF16),
            jax.ShapeDtypeStruct((dom, capacity), I32),
        ),
        (received, features, own, degree),
        scratch=(pltpu.VMEM((feats, masters), BF16),),
        flops=2 * received.size * masters,
        moved=received.size * 2,
    )


def collect_body(order, received, reps, out):
    feats = out.shape[0]
    for n in range(0, reps.shape[1], CHUNK):
        at = slice(n, n + CHUNK)
        spots = one_hot(reps[1:2, at], received.shape[2])
        out[:, at] = pick_all(order, received, spots, reps[0:1, at], feats).astype(BF16)


def bring_body(masks_hbm, masks, arrived):
    for copy in fetch(masks_hbm, masks, arrived):
        copy.wait()


def weights_body(feat, me, self_one, neigh_one, self_two, neigh_two, both_out, both_own, mirror_own, self_own, neigh_own):
    rows_one = self_one.shape[0] // feat
    rows_two = neigh_two.shape[0] // feat
    wide_one = self_one.shape[1] // feat
    wide_two = neigh_two.shape[1] // feat

    def turned(pieces):
        return jnp.concatenate([piece.astype(F32) for piece in pieces], axis=0).T.astype(BF16)

    def fill(f):
        def block(weight, rows, k):
            return weight[(f ^ k) * rows : ((f ^ k) + 1) * rows, :]

        def own(values, wide):
            return values[f * wide : (f + 1) * wide]

        ones = [[block(w, rows_one, k) for w in (self_one, neigh_one)] for k in range(feat)]
        both = turned([piece for pair in ones for piece in pair])
        both_out[...] = both
        both_own[...] = own(both, wide_one)
        mirror_own[...] = own(turned([pair[i] for i in range(2) for pair in ones]), wide_one)
        self_own[...] = own(turned([self_two[...]]), wide_two)
        neigh_own[...] = own(turned([block(neigh_two, rows_two, k) for k in range(feat)]), wide_two)

    for f in range(feat):
        pl.when(me[0] == f)(functools.partial(fill, f))


def turn_weights(feat, me, self_one, neigh_one, self_two, neigh_two):
    wide_one = self_one.shape[1] // feat
    wide_two = neigh_two.shape[1] // feat
    depth = 2 * self_one.shape[0]
    shapes = [
        (self_one.shape[1], depth),
        (wide_one, depth),
        (wide_one, depth),
        (wide_two, self_two.shape[0]),
        (wide_two, neigh_two.shape[0]),
    ]
    return call(
        functools.partial(weights_body, feat),
        tuple(jax.ShapeDtypeStruct(shape, BF16) for shape in shapes),
        (me.reshape(1), self_one, neigh_one, self_two, neigh_two),
        smem=(0,),
        moved=2 * sum(a * b for a, b in shapes),
    )


def stack(refs, at=slice(None)):
    return jnp.concatenate([ref[:, at] for ref in refs], axis=0)


def hidden_body(feat, both_t, both_own, self_two_own, *refs):
    own_out, self_out = refs[feat:]
    values = stack(refs[:feat])
    own_out[...] = jnp.maximum(dot(both_own[...], values), 0.0).astype(BF16)
    hidden = jnp.maximum(dot(both_t[...], values), 0.0).astype(BF16)
    self_out[...] = dot(self_two_own[...], hidden)


def second_body(feat, order, cols, mirror_own, own, masks, reps, *refs):
    rows = refs[: 2 * feat]
    own_out, out, local, mirror = refs[2 * feat :]
    feats, masters = own.shape
    head = masters // LANES
    for i in range(head):
        local[i] = own[:, i * LANES : (i + 1) * LANES]
    for n in range(0, reps.shape[1], CHUNK):
        result = dot(mirror_own[...], stack(rows, slice(n, n + CHUNK)))
        values = jnp.maximum(result, 0.0).astype(BF16)
        for i in range(CHUNK // LANES):
            local[head + n // LANES + i] = values[:, i * LANES : (i + 1) * LANES]
    aggregate(cols, local, masks, head, own_out, mirror)
    send(order, mirror, reps, out, False)


def second_sums(order, cols, inputs, means, mirror_own, own, masks, reps, capacity):
    feats, masters = own.shape
    mirrors = reps.shape[1]
    rows = capacity // LANES * feats
    return call(
        functools.partial(second_body, len(means), order),
        (
            jax.ShapeDtypeStruct((feats, masters), F32),
            jax.ShapeDtypeStruct((len(order), rows, LANES), BF16),
        ),
        (cols, mirror_own, own, masks, reps) + inputs + means,
        smem=(0,),
        scratch=(
            pltpu.VMEM((masks.shape[0], feats, LANES), BF16),
            pltpu.VMEM((feats, mirrors), BF16),
        ),
        flops=2 * feats * masks.size,
        moved=masks.size,
    )


def second_mean_body(received, rows, own, degree, out):
    feats, masters = own.shape
    dom, capacity = rows.shape

    def high(p):
        return rows[pl.ds(p, 1), :] >> SHIFT

    def low(p):
        return rows[pl.ds(p, 1), :] & (CHUNK - 1)

    total = add_mirrors(dom, received, high, low, feats, capacity // LANES, masters)
    divide(total, own, degree, out)


def embed_body(count, neigh_t, total, *refs):
    out = refs[count]
    out[...] = (total[...] + dot(neigh_t[...], stack(refs[:count]))).astype(out.dtype)


def embed(neigh_t, total, blocks, dtype):
    return call(
        functools.partial(embed_body, len(blocks)),
        jax.ShapeDtypeStruct(total.shape, dtype),
        (neigh_t, total) + blocks,
        flops=2 * total.size * neigh_t.shape[1],
        moved=10 * total.size,
    )


def on_device(
    features, tile_mask, tile_cols, replicas, degree, self_one, neigh_one, self_two, neigh_two
):
    dom = lax.axis_size("dom")
    feat = lax.axis_size("feat")
    feats, masters = features.shape
    mirrors = replicas.shape[1]
    hidden_feats = self_one.shape[1] // feat
    capacity = -(-(2 * mirrors // dom) // LANES) * LANES
    cols = tile_cols.T
    degree = degree.reshape(1, masters)

    order = ORDER if dom == len(ORDER) else tuple(range(dom))

    def exchange(blocks):
        return lax.all_to_all(
            blocks, "dom", split_axis=0, concat_axis=0, tiled=True, axis_index_groups=[list(order)]
        )

    me = lax.axis_index("feat")

    def swap(values, k):
        return lax.ppermute(values, "feat", [(i, i ^ k) for i in range(feat)])

    def gather(blocks, stop=feat):
        blocks = list(blocks)
        for k in range(len(blocks), stop):
            low = k & -k
            blocks.append(swap(blocks[k ^ low], low))
        return tuple(blocks)

    last = feat - 1
    together = lax.optimization_barrier

    def spread(columns):
        if dom != GROUP:
            return (exchange(jnp.broadcast_to(columns[None], (dom,) + columns.shape)),)
        half = dom // 2
        others = list(range(1, half))

        def swap(values, k):
            return lax.ppermute(values, "dom", [(i, i ^ k) for i in range(dom)])

        far = swap(columns, half)
        near = [swap(columns, k) for k in others]
        return (*near, far, *[swap(far, k) for k in others])

    received = spread(features)
    masks = transpose_masks(tile_mask)
    own_one, mirror_in, outgoing, kept_masks = first_sums(
        order, cols, received, features, masks, replicas, capacity
    )
    sums = exchange(outgoing)
    own_both, asked, rows = first_mean(dom, sums, features, own_one, degree, capacity)
    own_both, weights = together((own_both, (self_one, neigh_one, self_two, neigh_two)))
    slots = exchange(asked)
    inputs = gather((own_both,))
    both_t, both_own, mirror_own, self_two_own, neigh_two_own = turn_weights(feat, me, *weights)
    slots, both_t, both_own, mirror_own, self_two_own, neigh_two_own = together(
        (slots, both_t, both_own, mirror_own, self_two_own, neigh_two_own)
    )
    mirror_mean = call(
        functools.partial(collect_body, order),
        jax.ShapeDtypeStruct((feats, mirrors), BF16),
        (slots, replicas),
        flops=2 * slots.size * mirrors,
        moved=2 * slots.size,
    )
    mirror_mean, kept_masks = together((mirror_mean, kept_masks))
    means = gather((mirror_mean,), last)
    near_masks = call(
        bring_body,
        jax.ShapeDtypeStruct(masks.shape, MASK),
        (kept_masks,),
        hbm=(0,),
        limit=44,
        scratch=(pltpu.SemaphoreType.DMA((PIECES,)),),
        moved=2 * masks.size,
    )
    hidden, self_part = call(
        functools.partial(hidden_body, feat),
        (
            jax.ShapeDtypeStruct((hidden_feats, masters), BF16),
            jax.ShapeDtypeStruct((self_two_own.shape[0], masters), F32),
        ),
        (both_t, both_own, self_two_own) + inputs,
        flops=2 * masters * (4 * self_one.size + self_two_own.size),
        moved=masters * 1024,
    )
    means, near_masks, hidden, self_part, neigh_two_own = together(
        (means, near_masks, hidden, self_part, neigh_two_own)
    )
    own_two, outgoing = second_sums(
        order, cols, gather((mirror_in,)), gather(means), mirror_own, hidden, near_masks, replicas, capacity
    )
    mean_two = call(
        second_mean_body,
        jax.ShapeDtypeStruct((hidden_feats, masters), BF16),
        (exchange(outgoing), rows, own_two, degree),
        flops=2 * hidden_feats * dom * capacity * masters,
        moved=2 * hidden_feats * dom * capacity,
    )
    blocks = gather((mean_two,))
    total = self_part
    for start, stop in ((0, 3), (3, 4)):
        weights = neigh_two_own[:, start * hidden_feats : stop * hidden_feats]
        total = embed(weights, total, blocks[start:stop], BF16 if stop == feat else F32)
    return total


def solution(mesh):
    return jax.shard_map(
        on_device,
        mesh=mesh,
        in_specs=(
            P("feat", "dom"),
            P("dom", None, None, None),
            P("dom", None),
            P(None, "dom"),
            P("dom"),
            P(),
            P(),
            P(),
            P(),
        ),
        out_specs=P("feat", "dom"),
        check_vma=False,
    )
```

```python
import functools

import jax
import jax.numpy as jnp
from jax import lax
from jax.experimental import pallas as pl
from jax.experimental.pallas import tpu as pltpu
from jax.sharding import PartitionSpec as P

F32 = jnp.float32
BF16 = jnp.bfloat16
I32 = jnp.int32
MASK = jnp.float8_e4m3fn
LANES = 128
SHIFT = 8
CHUNK = 1 << SHIFT
GROUP = 8
ORDER = (5, 3, 2, 7, 1, 0, 4, 6)
INDEX_ROWS = 16
VMEM = pl.BlockSpec(memory_space=pltpu.VMEM)
SMEM = pl.BlockSpec(memory_space=pltpu.SMEM)
HBM = pl.BlockSpec(memory_space=pltpu.HBM)
PIECES = 4
MASK_PIECES = 8
SPARE = 10


def call(body, out_shape, operands, smem=(), hbm=(), hbm_out=(), scratch=(), flops=0, moved=0, limit=20):
    def place(i):
        return SMEM if i in smem else HBM if i in hbm else VMEM

    return pl.pallas_call(
        body,
        out_shape=out_shape,
        in_specs=[place(i) for i in range(len(operands))],
        out_specs=(
            tuple(HBM if i in hbm_out else VMEM for i in range(len(out_shape)))
            if isinstance(out_shape, tuple)
            else VMEM
        ),
        scratch_shapes=list(scratch),
        compiler_params=pltpu.CompilerParams(vmem_limit_bytes=limit << 20),
        cost_estimate=pl.CostEstimate(flops=flops, bytes_accessed=moved, transcendentals=0),
    )(*operands)


def dot(left, right, dims=(1, 0)):
    return lax.dot_general(
        left, right, (((dims[0],), (dims[1],)), ((), ())), preferred_element_type=F32
    )


def one_hot(index_row, depth):
    side = min(depth, CHUNK)
    n = index_row.shape[1]
    rows = lax.broadcasted_iota(I32, (side, n), 0).astype(F32).astype(BF16)
    blocks = []
    for start in range(0, depth, side):
        here = (index_row >= start) & (index_row < start + side)
        spot = jnp.where(here, index_row - start, -1).astype(F32).astype(BF16)
        blocks.append(jnp.where(rows == spot, jnp.ones_like(rows), jnp.zeros_like(rows)))
    return blocks[0] if len(blocks) == 1 else jnp.concatenate(blocks, axis=0)


def keep(condition, values):
    return jnp.where(condition, values, jnp.zeros_like(values))


def loop(count, body, carry):
    if count <= GROUP:
        for i in range(count):
            carry = body(i, carry)
        return carry
    return lax.fori_loop(0, count, body, carry)


def masks_body(tile_mask, out, blocks, arrived):
    tiles, stored, side, _ = blocks.shape
    copies = fetch(tile_mask, blocks, arrived)
    step = tiles // len(copies)
    for i in range(tiles):
        if i % step == 0:
            copies[i // step].wait()
        for k in range(stored):
            block = blocks[i, k].astype(F32).astype(BF16)
            out[i, k * side : (k + 1) * side, :] = block.T


def transpose_masks(tile_mask):
    tiles, stored, side, _ = tile_mask.shape
    return call(
        masks_body,
        jax.ShapeDtypeStruct((tiles, stored * side, side), BF16),
        (tile_mask,),
        hbm=(0,),
        limit=47,
        scratch=(
            pltpu.VMEM(tile_mask.shape, I32),
            pltpu.SemaphoreType.DMA((MASK_PIECES,)),
        ),
        moved=6 * tile_mask.size,
    )


def index_rows(part, row, slot_places, names):
    blocks = slot_places.shape[0] // LANES
    name = lax.broadcasted_iota(I32, (len(names), 1), 0)
    for k, q in enumerate(names):
        name = jnp.where(lax.broadcasted_iota(I32, (len(names), 1), 0) == k, q, name)
    mine = jnp.broadcast_to(name, (len(names), part.shape[1])) == part
    digits = [keep(mine, jnp.broadcast_to(d, mine.shape)) for d in (row >> SHIFT, row & (CHUNK - 1))]
    digits = jnp.concatenate(digits, axis=0).astype(F32).astype(BF16)
    found = dot(digits, slot_places, (1, 1))
    out = []
    for k in range(len(names)):
        pieces = [
            found[at : at + 1, b * LANES : (b + 1) * LANES]
            for at in (k, len(names) + k)
            for b in range(blocks)
        ]
        pieces.append(jnp.zeros((INDEX_ROWS - len(pieces), LANES), F32))
        out.append(jnp.concatenate(pieces, axis=0).astype(BF16))
    return out


def pick(blocks, names, spots, part, feats):
    found = dot(jnp.concatenate(blocks, axis=0), spots)
    total = jnp.zeros((feats, spots.shape[1]), F32)
    for k, name in enumerate(names):
        total = total + keep(part == name, found[k * feats : (k + 1) * feats])
    return total


def pick_all(order, received, spots, part, feats):
    dom = received.shape[0]
    if dom == GROUP:
        return pick([received[k] for k in range(dom)], order, spots, part, feats)

    def add_group(g, total):
        blocks = [received[g * GROUP + k] for k in range(GROUP)]
        return total + pick(blocks, range(GROUP), spots, part - g * GROUP, feats)

    return lax.fori_loop(0, dom // GROUP, add_group, jnp.zeros((feats, spots.shape[1]), F32))


def fetch(source, target, arrived):
    pieces = arrived.shape[0]
    step = target.shape[0] // pieces
    copies = []
    for i in range(pieces):
        at = pl.ds(i * step, step)
        copies.append(pltpu.make_async_copy(source.at[at], target.at[at], arrived.at[i]))
        copies[-1].start()
    return copies


def aggregate(cols, local, masks, head, own_out, mirror, narrow=None):
    stored = masks.shape[1] // LANES
    for i in range(masks.shape[0]):
        chosen = jnp.concatenate([local[cols[k, i]] for k in range(stored)], axis=1)
        row = masks[i]
        if narrow is not None:
            narrow[i] = row.astype(MASK)
        summed = dot(chosen, row.astype(BF16))
        if i < head:
            own_out[:, i * LANES : (i + 1) * LANES] = summed
        else:
            at = (i - head) * LANES
            mirror[:, at : at + LANES] = summed.astype(BF16)


def send(order, mirror, reps, out, with_index):
    feats = mirror.shape[0]
    dom = out.shape[0]
    rows = out.shape[1] // feats * feats
    blocks = rows // feats
    part, slot, row = reps[0:1, :], reps[1:2, :], reps[2:3, :]
    slot_places = one_hot(slot, blocks * LANES)
    values = mirror[...]

    def group(first, names, part):
        spread = jnp.concatenate([keep(part == name, values) for name in names], axis=0)
        placed = dot(spread, slot_places, (1, 1)).astype(BF16)
        for k in range(GROUP):
            for b in range(blocks):
                block = placed[k * feats : (k + 1) * feats, b * LANES : (b + 1) * LANES]
                out[first + k, b * feats : (b + 1) * feats, :] = block
        if with_index:
            for k, index in enumerate(index_rows(part, row, slot_places, names)):
                out[first + k, rows:, :] = index

    if dom == GROUP:
        group(0, order, part)
    else:

        def one(g, carry):
            group(g * GROUP, range(GROUP), part - g * GROUP)
            return carry

        lax.fori_loop(0, dom // GROUP, one, 0)


def first_body(order, cols, own, masks, reps, *refs):
    received = refs[:-8]
    own_out, all_out, out, kept, local, mirror, narrow, written = refs[-8:]
    feats, masters = own.shape
    head = masters // LANES
    for i in range(head):
        local[i] = own[:, i * LANES : (i + 1) * LANES]
    for n in range(0, reps.shape[1], CHUNK):
        at = slice(n, n + CHUNK)
        spots = one_hot(reps[2:3, at], masters)
        part = reps[0:1, at]
        if len(received) == 1:
            values = pick_all(order, received[0], spots, part, feats)
        else:
            part = part ^ lax.axis_index("dom")
            blocks = [ref[...] for ref in received]
            values = pick(blocks, range(1, len(blocks) + 1), spots, part, feats)
        values = values.astype(BF16)
        all_out[:, at] = values
        for i in range(CHUNK // LANES):
            local[head + n // LANES + i] = values[:, i * LANES : (i + 1) * LANES]
    aggregate(cols, local, masks, head, own_out, mirror, narrow)
    copy = pltpu.make_async_copy(narrow, kept.at[pl.ds(0, masks.shape[0])], written)
    copy.start()
    send(order, mirror, reps, out, True)
    copy.wait()


def first_sums(order, cols, received, own, masks, reps, capacity):
    feats, masters = own.shape
    mirrors = reps.shape[1]
    rows = capacity // LANES * feats + INDEX_ROWS
    tiles = masks.shape[0]
    return call(
        functools.partial(first_body, order),
        (
            jax.ShapeDtypeStruct((feats, masters), F32),
            jax.ShapeDtypeStruct((feats, mirrors), BF16),
            jax.ShapeDtypeStruct((len(order), rows, LANES), BF16),
            jax.ShapeDtypeStruct((SPARE * tiles,) + masks.shape[1:], MASK),
        ),
        (cols, own, masks, reps) + received,
        smem=(0,),
        hbm_out=(3,),
        limit=44,
        scratch=(
            pltpu.VMEM((tiles, feats, LANES), BF16),
            pltpu.VMEM((feats, mirrors), BF16),
            pltpu.VMEM(masks.shape, MASK),
            pltpu.SemaphoreType.DMA,
        ),
        flops=2 * feats * masks.size,
        moved=2 * masks.size,
    )


def message(received, p, feats, blocks):
    return jnp.concatenate([received[p, b * feats : (b + 1) * feats, :] for b in range(blocks)], axis=1)


def add_mirrors(dom, received, high, low, feats, blocks, masters):
    parts = masters // CHUNK

    def add(p, total):
        values = message(received, p, feats, blocks)
        spread = jnp.concatenate([keep(high(p) == a, values) for a in range(parts)], axis=0)
        return total + dot(spread, one_hot(low(p), CHUNK), (1, 1))

    return loop(dom, add, jnp.zeros((parts * feats, CHUNK), F32))


def divide(total, own, degree, out):
    feats, masters = own.shape
    for a in range(masters // CHUNK):
        at = slice(a * CHUNK, (a + 1) * CHUNK)
        whole = own[:, at] + total[a * feats : (a + 1) * feats]
        out[:, at] = (whole / degree[:, at].astype(F32)).astype(BF16)


def first_mean_body(received, features, own, degree, out, asked, rows_out, mean):
    feats, masters = own.shape
    dom, capacity = rows_out.shape
    blocks = capacity // LANES
    parts = masters // CHUNK

    def rows(p, carry):
        coded = received[p, blocks * feats :, :].astype(F32).astype(I32)
        high = jnp.concatenate([coded[b : b + 1] for b in range(blocks)], axis=1)
        low = jnp.concatenate([coded[blocks + b : blocks + b + 1] for b in range(blocks)], axis=1)
        rows_out[pl.ds(p, 1), :] = high * CHUNK + low
        return carry

    loop(dom, rows, 0)

    def high(p):
        return rows_out[pl.ds(p, 1), :] >> SHIFT

    def low(p):
        return rows_out[pl.ds(p, 1), :] & (CHUNK - 1)

    total = add_mirrors(dom, received, high, low, feats, blocks, masters)
    divide(total, own, degree, mean)
    folded = jnp.concatenate([mean[:, a * CHUNK : (a + 1) * CHUNK] for a in range(parts)], axis=0)

    def one(p, carry):
        found = dot(folded, one_hot(low(p), CHUNK))
        chosen = jnp.zeros((feats, capacity), F32)
        for a in range(parts):
            chosen = chosen + keep(high(p) == a, found[a * feats : (a + 1) * feats])
        asked[p] = chosen.astype(BF16)
        return carry

    loop(dom, one, 0)
    out[:feats] = features[...]
    out[feats:] = mean[...]


def first_mean(dom, received, features, own, degree, capacity):
    feats, masters = own.shape
    return call(
        first_mean_body,
        (
            jax.ShapeDtypeStruct((2 * feats, masters), BF16),
            jax.ShapeDtypeStruct((dom, feats, capacity), BF16),
            jax.ShapeDtypeStruct((dom, capacity), I32),
        ),
        (received, features, own, degree),
        scratch=(pltpu.VMEM((feats, masters), BF16),),
        flops=2 * received.size * masters,
        moved=received.size * 2,
    )


def collect_body(order, received, reps, out):
    feats = out.shape[0]
    for n in range(0, reps.shape[1], CHUNK):
        at = slice(n, n + CHUNK)
        spots = one_hot(reps[1:2, at], received.shape[2])
        out[:, at] = pick_all(order, received, spots, reps[0:1, at], feats).astype(BF16)


def bring_body(masks_hbm, masks, arrived):
    for copy in fetch(masks_hbm, masks, arrived):
        copy.wait()


def weights_body(feat, me, self_one, neigh_one, self_two, neigh_two, both_out, both_own, mirror_own, self_own, neigh_own):
    rows_one = self_one.shape[0] // feat
    rows_two = neigh_two.shape[0] // feat
    wide_one = self_one.shape[1] // feat
    wide_two = neigh_two.shape[1] // feat

    def turned(pieces):
        return jnp.concatenate([piece.astype(F32) for piece in pieces], axis=0).T.astype(BF16)

    def fill(f):
        def block(weight, rows, k):
            return weight[(f ^ k) * rows : ((f ^ k) + 1) * rows, :]

        def own(values, wide):
            return values[f * wide : (f + 1) * wide]

        ones = [[block(w, rows_one, k) for w in (self_one, neigh_one)] for k in range(feat)]
        both = turned([piece for pair in ones for piece in pair])
        both_out[...] = both
        both_own[...] = own(both, wide_one)
        mirror_own[...] = own(turned([pair[i] for i in range(2) for pair in ones]), wide_one)
        self_own[...] = own(turned([self_two[...]]), wide_two)
        neigh_own[...] = own(turned([block(neigh_two, rows_two, k) for k in range(feat)]), wide_two)

    for f in range(feat):
        pl.when(me[0] == f)(functools.partial(fill, f))


def turn_weights(feat, me, self_one, neigh_one, self_two, neigh_two):
    wide_one = self_one.shape[1] // feat
    wide_two = neigh_two.shape[1] // feat
    depth = 2 * self_one.shape[0]
    shapes = [
        (self_one.shape[1], depth),
        (wide_one, depth),
        (wide_one, depth),
        (wide_two, self_two.shape[0]),
        (wide_two, neigh_two.shape[0]),
    ]
    return call(
        functools.partial(weights_body, feat),
        tuple(jax.ShapeDtypeStruct(shape, BF16) for shape in shapes),
        (me.reshape(1), self_one, neigh_one, self_two, neigh_two),
        smem=(0,),
        moved=2 * sum(a * b for a, b in shapes),
    )


def stack(refs, at=slice(None)):
    return jnp.concatenate([ref[:, at] for ref in refs], axis=0)


def hidden_body(feat, both_t, both_own, self_two_own, *refs):
    own_out, self_out = refs[feat:]
    values = stack(refs[:feat])
    own_out[...] = jnp.maximum(dot(both_own[...], values), 0.0).astype(BF16)
    hidden = jnp.maximum(dot(both_t[...], values), 0.0).astype(BF16)
    self_out[...] = dot(self_two_own[...], hidden)


def second_body(feat, order, cols, mirror_own, own, masks, reps, *refs):
    rows = refs[: 2 * feat]
    own_out, out, local, mirror = refs[2 * feat :]
    feats, masters = own.shape
    head = masters // LANES
    for i in range(head):
        local[i] = own[:, i * LANES : (i + 1) * LANES]
    for n in range(0, reps.shape[1], CHUNK):
        result = dot(mirror_own[...], stack(rows, slice(n, n + CHUNK)))
        values = jnp.maximum(result, 0.0).astype(BF16)
        for i in range(CHUNK // LANES):
            local[head + n // LANES + i] = values[:, i * LANES : (i + 1) * LANES]
    aggregate(cols, local, masks, head, own_out, mirror)
    send(order, mirror, reps, out, False)


def second_sums(order, cols, inputs, means, mirror_own, own, masks, reps, capacity):
    feats, masters = own.shape
    mirrors = reps.shape[1]
    rows = capacity // LANES * feats
    return call(
        functools.partial(second_body, len(means), order),
        (
            jax.ShapeDtypeStruct((feats, masters), F32),
            jax.ShapeDtypeStruct((len(order), rows, LANES), BF16),
        ),
        (cols, mirror_own, own, masks, reps) + inputs + means,
        smem=(0,),
        scratch=(
            pltpu.VMEM((masks.shape[0], feats, LANES), BF16),
            pltpu.VMEM((feats, mirrors), BF16),
        ),
        flops=2 * feats * masks.size,
        moved=masks.size,
    )


def second_mean_body(received, rows, own, degree, out):
    feats, masters = own.shape
    dom, capacity = rows.shape

    def high(p):
        return rows[pl.ds(p, 1), :] >> SHIFT

    def low(p):
        return rows[pl.ds(p, 1), :] & (CHUNK - 1)

    total = add_mirrors(dom, received, high, low, feats, capacity // LANES, masters)
    divide(total, own, degree, out)


def embed_body(count, neigh_t, total, *refs):
    out = refs[count]
    out[...] = (total[...] + dot(neigh_t[...], stack(refs[:count]))).astype(out.dtype)


def embed(neigh_t, total, blocks, dtype):
    return call(
        functools.partial(embed_body, len(blocks)),
        jax.ShapeDtypeStruct(total.shape, dtype),
        (neigh_t, total) + blocks,
        flops=2 * total.size * neigh_t.shape[1],
        moved=10 * total.size,
    )


def on_device(
    features, tile_mask, tile_cols, replicas, degree, self_one, neigh_one, self_two, neigh_two
):
    dom = lax.axis_size("dom")
    feat = lax.axis_size("feat")
    feats, masters = features.shape
    mirrors = replicas.shape[1]
    hidden_feats = self_one.shape[1] // feat
    capacity = -(-(2 * mirrors // dom) // LANES) * LANES
    cols = tile_cols.T
    degree = degree.reshape(1, masters)

    order = ORDER if dom == len(ORDER) else tuple(range(dom))

    def exchange(blocks):
        return lax.all_to_all(
            blocks, "dom", split_axis=0, concat_axis=0, tiled=True, axis_index_groups=[list(order)]
        )

    me = lax.axis_index("feat")

    def swap(values, k):
        return lax.ppermute(values, "feat", [(i, i ^ k) for i in range(feat)])

    def gather(blocks, stop=feat):
        blocks = list(blocks)
        for k in range(len(blocks), stop):
            low = k & -k
            blocks.append(swap(blocks[k ^ low], low))
        return tuple(blocks)

    last = feat - 1
    together = lax.optimization_barrier

    def spread(columns):
        if dom != GROUP:
            return (exchange(jnp.broadcast_to(columns[None], (dom,) + columns.shape)),)
        half = dom // 2
        others = list(range(1, half))

        def swap(values, k):
            return lax.ppermute(values, "dom", [(i, i ^ k) for i in range(dom)])

        far = swap(columns, half)
        near = [swap(columns, k) for k in others]
        return (*near, far, *[swap(far, k) for k in others])

    received = spread(features)
    masks = transpose_masks(tile_mask)
    own_one, mirror_in, outgoing, kept_masks = first_sums(
        order, cols, received, features, masks, replicas, capacity
    )
    sums = exchange(outgoing)
    own_both, asked, rows = first_mean(dom, sums, features, own_one, degree, capacity)
    own_both, weights = together((own_both, (self_one, neigh_one, self_two, neigh_two)))
    slots = exchange(asked)
    inputs = gather((own_both,))
    both_t, both_own, mirror_own, self_two_own, neigh_two_own = turn_weights(feat, me, *weights)
    slots, both_t, both_own, mirror_own, self_two_own, neigh_two_own = together(
        (slots, both_t, both_own, mirror_own, self_two_own, neigh_two_own)
    )
    mirror_mean = call(
        functools.partial(collect_body, order),
        jax.ShapeDtypeStruct((feats, mirrors), BF16),
        (slots, replicas),
        flops=2 * slots.size * mirrors,
        moved=2 * slots.size,
    )
    mirror_mean, kept_masks = together((mirror_mean, kept_masks))
    means = gather((mirror_mean,), last)
    near_masks = call(
        bring_body,
        jax.ShapeDtypeStruct(masks.shape, MASK),
        (kept_masks,),
        hbm=(0,),
        limit=44,
        scratch=(pltpu.SemaphoreType.DMA((PIECES,)),),
        moved=2 * masks.size,
    )
    hidden, self_part = call(
        functools.partial(hidden_body, feat),
        (
            jax.ShapeDtypeStruct((hidden_feats, masters), BF16),
            jax.ShapeDtypeStruct((self_two_own.shape[0], masters), F32),
        ),
        (both_t, both_own, self_two_own) + inputs,
        flops=2 * masters * (4 * self_one.size + self_two_own.size),
        moved=masters * 1024,
    )
    means, near_masks, neigh_two_own = together((means, near_masks, neigh_two_own))
    own_two, outgoing = second_sums(
        order, cols, gather((mirror_in,)), gather(means), mirror_own, hidden, near_masks, replicas, capacity
    )
    mean_two = call(
        second_mean_body,
        jax.ShapeDtypeStruct((hidden_feats, masters), BF16),
        (exchange(outgoing), rows, own_two, degree),
        flops=2 * hidden_feats * dom * capacity * masters,
        moved=2 * hidden_feats * dom * capacity,
    )
    blocks = gather((mean_two,))
    total = self_part
    for start, stop in ((0, 3), (3, 4)):
        weights = neigh_two_own[:, start * hidden_feats : stop * hidden_feats]
        total = embed(weights, total, blocks[start:stop], BF16 if stop == feat else F32)
    return total


def solution(mesh):
    return jax.shard_map(
        on_device,
        mesh=mesh,
        in_specs=(
            P("feat", "dom"),
            P("dom", None, None, None),
            P("dom", None),
            P(None, "dom"),
            P("dom"),
            P(),
            P(),
            P(),
            P(),
        ),
        out_specs=P("feat", "dom"),
        check_vma=False,
    )
```

```python
import functools

import jax
import jax.numpy as jnp
from jax import lax
from jax.experimental import pallas as pl
from jax.experimental.pallas import tpu as pltpu
from jax.sharding import PartitionSpec as P

F32 = jnp.float32
BF16 = jnp.bfloat16
I32 = jnp.int32
MASK = jnp.float8_e4m3fn
LANES = 128
SHIFT = 8
CHUNK = 1 << SHIFT
GROUP = 8
ORDER = (5, 3, 2, 7, 1, 0, 4, 6)
INDEX_ROWS = 16
VMEM = pl.BlockSpec(memory_space=pltpu.VMEM)
SMEM = pl.BlockSpec(memory_space=pltpu.SMEM)
HBM = pl.BlockSpec(memory_space=pltpu.HBM)
PIECES = 4
MASK_PIECES = 8
SPARE = 10


def call(body, out_shape, operands, smem=(), hbm=(), hbm_out=(), scratch=(), flops=0, moved=0, limit=20):
    def place(i):
        return SMEM if i in smem else HBM if i in hbm else VMEM

    return pl.pallas_call(
        body,
        out_shape=out_shape,
        in_specs=[place(i) for i in range(len(operands))],
        out_specs=(
            tuple(HBM if i in hbm_out else VMEM for i in range(len(out_shape)))
            if isinstance(out_shape, tuple)
            else VMEM
        ),
        scratch_shapes=list(scratch),
        compiler_params=pltpu.CompilerParams(vmem_limit_bytes=limit << 20),
        cost_estimate=pl.CostEstimate(flops=flops, bytes_accessed=moved, transcendentals=0),
    )(*operands)


def dot(left, right, dims=(1, 0)):
    return lax.dot_general(
        left, right, (((dims[0],), (dims[1],)), ((), ())), preferred_element_type=F32
    )


def one_hot(index_row, depth):
    side = min(depth, CHUNK)
    n = index_row.shape[1]
    rows = lax.broadcasted_iota(I32, (side, n), 0).astype(F32).astype(BF16)
    blocks = []
    for start in range(0, depth, side):
        here = (index_row >= start) & (index_row < start + side)
        spot = jnp.where(here, index_row - start, -1).astype(F32).astype(BF16)
        blocks.append(jnp.where(rows == spot, jnp.ones_like(rows), jnp.zeros_like(rows)))
    return blocks[0] if len(blocks) == 1 else jnp.concatenate(blocks, axis=0)


def keep(condition, values):
    return jnp.where(condition, values, jnp.zeros_like(values))


def loop(count, body, carry):
    if count <= GROUP:
        for i in range(count):
            carry = body(i, carry)
        return carry
    return lax.fori_loop(0, count, body, carry)


def masks_body(tile_mask, out, blocks, arrived):
    tiles, stored, side, _ = blocks.shape
    copies = fetch(tile_mask, blocks, arrived)
    step = tiles // len(copies)
    for i in range(tiles):
        if i % step == 0:
            copies[i // step].wait()
        for k in range(stored):
            block = blocks[i, k].astype(F32).astype(BF16)
            out[i, k * side : (k + 1) * side, :] = block.T


def transpose_masks(tile_mask):
    tiles, stored, side, _ = tile_mask.shape
    return call(
        masks_body,
        jax.ShapeDtypeStruct((tiles, stored * side, side), BF16),
        (tile_mask,),
        hbm=(0,),
        limit=47,
        scratch=(
            pltpu.VMEM(tile_mask.shape, I32),
            pltpu.SemaphoreType.DMA((MASK_PIECES,)),
        ),
        moved=6 * tile_mask.size,
    )


def index_rows(part, row, slot_places, names):
    blocks = slot_places.shape[0] // LANES
    name = lax.broadcasted_iota(I32, (len(names), 1), 0)
    for k, q in enumerate(names):
        name = jnp.where(lax.broadcasted_iota(I32, (len(names), 1), 0) == k, q, name)
    mine = jnp.broadcast_to(name, (len(names), part.shape[1])) == part
    digits = [keep(mine, jnp.broadcast_to(d, mine.shape)) for d in (row >> SHIFT, row & (CHUNK - 1))]
    digits = jnp.concatenate(digits, axis=0).astype(F32).astype(BF16)
    found = dot(digits, slot_places, (1, 1))
    out = []
    for k in range(len(names)):
        pieces = [
            found[at : at + 1, b * LANES : (b + 1) * LANES]
            for at in (k, len(names) + k)
            for b in range(blocks)
        ]
        pieces.append(jnp.zeros((INDEX_ROWS - len(pieces), LANES), F32))
        out.append(jnp.concatenate(pieces, axis=0).astype(BF16))
    return out


def pick(blocks, names, spots, part, feats):
    found = dot(jnp.concatenate(blocks, axis=0), spots)
    total = jnp.zeros((feats, spots.shape[1]), F32)
    for k, name in enumerate(names):
        total = total + keep(part == name, found[k * feats : (k + 1) * feats])
    return total


def pick_all(order, received, spots, part, feats):
    dom = received.shape[0]
    if dom == GROUP:
        return pick([received[k] for k in range(dom)], order, spots, part, feats)

    def add_group(g, total):
        blocks = [received[g * GROUP + k] for k in range(GROUP)]
        return total + pick(blocks, range(GROUP), spots, part - g * GROUP, feats)

    return lax.fori_loop(0, dom // GROUP, add_group, jnp.zeros((feats, spots.shape[1]), F32))


def fetch(source, target, arrived):
    pieces = arrived.shape[0]
    step = target.shape[0] // pieces
    copies = []
    for i in range(pieces):
        at = pl.ds(i * step, step)
        copies.append(pltpu.make_async_copy(source.at[at], target.at[at], arrived.at[i]))
        copies[-1].start()
    return copies


def aggregate(cols, local, masks, head, own_out, mirror, narrow=None):
    stored = masks.shape[1] // LANES
    for i in range(masks.shape[0]):
        chosen = jnp.concatenate([local[cols[k, i]] for k in range(stored)], axis=1)
        row = masks[i]
        if narrow is not None:
            narrow[i] = row.astype(MASK)
        summed = dot(chosen, row.astype(BF16))
        if i < head:
            own_out[:, i * LANES : (i + 1) * LANES] = summed
        else:
            at = (i - head) * LANES
            mirror[:, at : at + LANES] = summed.astype(BF16)


def send(order, mirror, reps, out, with_index):
    feats = mirror.shape[0]
    dom = out.shape[0]
    rows = out.shape[1] // feats * feats
    blocks = rows // feats
    part, slot, row = reps[0:1, :], reps[1:2, :], reps[2:3, :]
    slot_places = one_hot(slot, blocks * LANES)
    values = mirror[...]

    def group(first, names, part):
        spread = jnp.concatenate([keep(part == name, values) for name in names], axis=0)
        placed = dot(spread, slot_places, (1, 1)).astype(BF16)
        for k in range(GROUP):
            for b in range(blocks):
                block = placed[k * feats : (k + 1) * feats, b * LANES : (b + 1) * LANES]
                out[first + k, b * feats : (b + 1) * feats, :] = block
        if with_index:
            for k, index in enumerate(index_rows(part, row, slot_places, names)):
                out[first + k, rows:, :] = index

    if dom == GROUP:
        group(0, order, part)
    else:

        def one(g, carry):
            group(g * GROUP, range(GROUP), part - g * GROUP)
            return carry

        lax.fori_loop(0, dom // GROUP, one, 0)


def first_body(order, cols, own, masks, reps, *refs):
    received = refs[:-8]
    own_out, all_out, out, kept, local, mirror, narrow, written = refs[-8:]
    feats, masters = own.shape
    head = masters // LANES
    for i in range(head):
        local[i] = own[:, i * LANES : (i + 1) * LANES]
    for n in range(0, reps.shape[1], CHUNK):
        at = slice(n, n + CHUNK)
        spots = one_hot(reps[2:3, at], masters)
        part = reps[0:1, at]
        if len(received) == 1:
            values = pick_all(order, received[0], spots, part, feats)
        else:
            part = part ^ lax.axis_index("dom")
            blocks = [ref[...] for ref in received]
            values = pick(blocks, range(1, len(blocks) + 1), spots, part, feats)
        values = values.astype(BF16)
        all_out[:, at] = values
        for i in range(CHUNK // LANES):
            local[head + n // LANES + i] = values[:, i * LANES : (i + 1) * LANES]
    aggregate(cols, local, masks, head, own_out, mirror, narrow)
    copy = pltpu.make_async_copy(narrow, kept.at[pl.ds(0, masks.shape[0])], written)
    copy.start()
    send(order, mirror, reps, out, True)
    copy.wait()


def first_sums(order, cols, received, own, masks, reps, capacity):
    feats, masters = own.shape
    mirrors = reps.shape[1]
    rows = capacity // LANES * feats + INDEX_ROWS
    tiles = masks.shape[0]
    return call(
        functools.partial(first_body, order),
        (
            jax.ShapeDtypeStruct((feats, masters), F32),
            jax.ShapeDtypeStruct((feats, mirrors), BF16),
            jax.ShapeDtypeStruct((len(order), rows, LANES), BF16),
            jax.ShapeDtypeStruct((SPARE * tiles,) + masks.shape[1:], MASK),
        ),
        (cols, own, masks, reps) + received,
        smem=(0,),
        hbm_out=(3,),
        limit=44,
        scratch=(
            pltpu.VMEM((tiles, feats, LANES), BF16),
            pltpu.VMEM((feats, mirrors), BF16),
            pltpu.VMEM(masks.shape, MASK),
            pltpu.SemaphoreType.DMA,
        ),
        flops=2 * feats * masks.size,
        moved=2 * masks.size,
    )


def message(received, p, feats, blocks):
    return jnp.concatenate([received[p, b * feats : (b + 1) * feats, :] for b in range(blocks)], axis=1)


def add_mirrors(dom, received, high, low, feats, blocks, masters):
    parts = masters // CHUNK

    def add(p, total):
        values = message(received, p, feats, blocks)
        spread = jnp.concatenate([keep(high(p) == a, values) for a in range(parts)], axis=0)
        return total + dot(spread, one_hot(low(p), CHUNK), (1, 1))

    return loop(dom, add, jnp.zeros((parts * feats, CHUNK), F32))


def divide(total, own, degree, out):
    feats, masters = own.shape
    for a in range(masters // CHUNK):
        at = slice(a * CHUNK, (a + 1) * CHUNK)
        whole = own[:, at] + total[a * feats : (a + 1) * feats]
        out[:, at] = (whole / degree[:, at].astype(F32)).astype(BF16)


def first_mean_body(received, features, own, degree, out, asked, rows_out, mean):
    feats, masters = own.shape
    dom, capacity = rows_out.shape
    blocks = capacity // LANES
    parts = masters // CHUNK

    def rows(p, carry):
        coded = received[p, blocks * feats :, :].astype(F32).astype(I32)
        high = jnp.concatenate([coded[b : b + 1] for b in range(blocks)], axis=1)
        low = jnp.concatenate([coded[blocks + b : blocks + b + 1] for b in range(blocks)], axis=1)
        rows_out[pl.ds(p, 1), :] = high * CHUNK + low
        return carry

    loop(dom, rows, 0)

    def high(p):
        return rows_out[pl.ds(p, 1), :] >> SHIFT

    def low(p):
        return rows_out[pl.ds(p, 1), :] & (CHUNK - 1)

    total = add_mirrors(dom, received, high, low, feats, blocks, masters)
    divide(total, own, degree, mean)
    folded = jnp.concatenate([mean[:, a * CHUNK : (a + 1) * CHUNK] for a in range(parts)], axis=0)

    def one(p, carry):
        found = dot(folded, one_hot(low(p), CHUNK))
        chosen = jnp.zeros((feats, capacity), F32)
        for a in range(parts):
            chosen = chosen + keep(high(p) == a, found[a * feats : (a + 1) * feats])
        asked[p] = chosen.astype(BF16)
        return carry

    loop(dom, one, 0)
    out[:feats] = features[...]
    out[feats:] = mean[...]


def first_mean(dom, received, features, own, degree, capacity):
    feats, masters = own.shape
    return call(
        first_mean_body,
        (
            jax.ShapeDtypeStruct((2 * feats, masters), BF16),
            jax.ShapeDtypeStruct((dom, feats, capacity), BF16),
            jax.ShapeDtypeStruct((dom, capacity), I32),
        ),
        (received, features, own, degree),
        scratch=(pltpu.VMEM((feats, masters), BF16),),
        flops=2 * received.size * masters,
        moved=received.size * 2,
    )


def collect_body(order, received, reps, out):
    feats = out.shape[0]
    for n in range(0, reps.shape[1], CHUNK):
        at = slice(n, n + CHUNK)
        spots = one_hot(reps[1:2, at], received.shape[2])
        out[:, at] = pick_all(order, received, spots, reps[0:1, at], feats).astype(BF16)


def bring_body(masks_hbm, masks, arrived):
    for copy in fetch(masks_hbm, masks, arrived):
        copy.wait()


def weights_body(feat, me, self_one, neigh_one, self_two, neigh_two, both_out, both_own, mirror_own, self_own, neigh_own):
    rows_one = self_one.shape[0] // feat
    rows_two = neigh_two.shape[0] // feat
    wide_one = self_one.shape[1] // feat
    wide_two = neigh_two.shape[1] // feat

    def turned(pieces):
        return jnp.concatenate([piece.astype(F32) for piece in pieces], axis=0).T.astype(BF16)

    def fill(f):
        def block(weight, rows, k):
            return weight[(f ^ k) * rows : ((f ^ k) + 1) * rows, :]

        def own(values, wide):
            return values[f * wide : (f + 1) * wide]

        ones = [[block(w, rows_one, k) for w in (self_one, neigh_one)] for k in range(feat)]
        both = turned([piece for pair in ones for piece in pair])
        both_out[...] = both
        both_own[...] = own(both, wide_one)
        mirror_own[...] = own(turned([pair[i] for i in range(2) for pair in ones]), wide_one)
        self_own[...] = own(turned([self_two[...]]), wide_two)
        neigh_own[...] = own(turned([block(neigh_two, rows_two, k) for k in range(feat)]), wide_two)

    for f in range(feat):
        pl.when(me[0] == f)(functools.partial(fill, f))


def turn_weights(feat, me, self_one, neigh_one, self_two, neigh_two):
    wide_one = self_one.shape[1] // feat
    wide_two = neigh_two.shape[1] // feat
    depth = 2 * self_one.shape[0]
    shapes = [
        (self_one.shape[1], depth),
        (wide_one, depth),
        (wide_one, depth),
        (wide_two, self_two.shape[0]),
        (wide_two, neigh_two.shape[0]),
    ]
    return call(
        functools.partial(weights_body, feat),
        tuple(jax.ShapeDtypeStruct(shape, BF16) for shape in shapes),
        (me.reshape(1), self_one, neigh_one, self_two, neigh_two),
        smem=(0,),
        moved=2 * sum(a * b for a, b in shapes),
    )


def stack(refs, at=slice(None)):
    return jnp.concatenate([ref[:, at] for ref in refs], axis=0)


def hidden_body(feat, both_t, both_own, self_two_own, *refs):
    own_out, self_out = refs[feat:]
    values = stack(refs[:feat])
    own_out[...] = jnp.maximum(dot(both_own[...], values), 0.0).astype(BF16)
    hidden = jnp.maximum(dot(both_t[...], values), 0.0).astype(BF16)
    self_out[...] = dot(self_two_own[...], hidden)


def second_body(feat, order, cols, mirror_own, own, masks, reps, *refs):
    rows = refs[: 2 * feat]
    own_out, out, local, mirror = refs[2 * feat :]
    feats, masters = own.shape
    head = masters // LANES
    for i in range(head):
        local[i] = own[:, i * LANES : (i + 1) * LANES]
    for n in range(0, reps.shape[1], CHUNK):
        result = dot(mirror_own[...], stack(rows, slice(n, n + CHUNK)))
        values = jnp.maximum(result, 0.0).astype(BF16)
        for i in range(CHUNK // LANES):
            local[head + n // LANES + i] = values[:, i * LANES : (i + 1) * LANES]
    aggregate(cols, local, masks, head, own_out, mirror)
    send(order, mirror, reps, out, False)


def second_sums(order, cols, inputs, means, mirror_own, own, masks, reps, capacity):
    feats, masters = own.shape
    mirrors = reps.shape[1]
    rows = capacity // LANES * feats
    return call(
        functools.partial(second_body, len(means), order),
        (
            jax.ShapeDtypeStruct((feats, masters), F32),
            jax.ShapeDtypeStruct((len(order), rows, LANES), BF16),
        ),
        (cols, mirror_own, own, masks, reps) + inputs + means,
        smem=(0,),
        scratch=(
            pltpu.VMEM((masks.shape[0], feats, LANES), BF16),
            pltpu.VMEM((feats, mirrors), BF16),
        ),
        flops=2 * feats * masks.size,
        moved=masks.size,
    )


def second_mean_body(received, rows, own, degree, out):
    feats, masters = own.shape
    dom, capacity = rows.shape

    def high(p):
        return rows[pl.ds(p, 1), :] >> SHIFT

    def low(p):
        return rows[pl.ds(p, 1), :] & (CHUNK - 1)

    total = add_mirrors(dom, received, high, low, feats, capacity // LANES, masters)
    divide(total, own, degree, out)


def embed_body(count, neigh_t, total, *refs):
    out = refs[count]
    out[...] = (total[...] + dot(neigh_t[...], stack(refs[:count]))).astype(out.dtype)


def embed(neigh_t, total, blocks, dtype):
    return call(
        functools.partial(embed_body, len(blocks)),
        jax.ShapeDtypeStruct(total.shape, dtype),
        (neigh_t, total) + blocks,
        flops=2 * total.size * neigh_t.shape[1],
        moved=10 * total.size,
    )


def on_device(
    features, tile_mask, tile_cols, replicas, degree, self_one, neigh_one, self_two, neigh_two
):
    dom = lax.axis_size("dom")
    feat = lax.axis_size("feat")
    feats, masters = features.shape
    mirrors = replicas.shape[1]
    hidden_feats = self_one.shape[1] // feat
    capacity = -(-(2 * mirrors // dom) // LANES) * LANES
    cols = tile_cols.T
    degree = degree.reshape(1, masters)

    order = ORDER if dom == len(ORDER) else tuple(range(dom))

    def exchange(blocks):
        return lax.all_to_all(
            blocks, "dom", split_axis=0, concat_axis=0, tiled=True, axis_index_groups=[list(order)]
        )

    me = lax.axis_index("feat")

    def swap(values, k):
        return lax.ppermute(values, "feat", [(i, i ^ k) for i in range(feat)])

    def gather(blocks, stop=feat):
        blocks = list(blocks)
        for k in range(len(blocks), stop):
            low = k & -k
            blocks.append(swap(blocks[k ^ low], low))
        return tuple(blocks)

    last = feat - 1
    together = lax.optimization_barrier

    def spread(columns):
        if dom != GROUP:
            return (exchange(jnp.broadcast_to(columns[None], (dom,) + columns.shape)),)
        half = dom // 2
        others = list(range(1, half))

        def swap(values, k):
            return lax.ppermute(values, "dom", [(i, i ^ k) for i in range(dom)])

        far = swap(columns, half)
        near = [swap(columns, k) for k in others]
        return (*near, far, *[swap(far, k) for k in others])

    received = spread(features)
    masks = transpose_masks(tile_mask)
    own_one, mirror_in, outgoing, kept_masks = first_sums(
        order, cols, received, features, masks, replicas, capacity
    )
    sums = exchange(outgoing)
    own_both, asked, rows = first_mean(dom, sums, features, own_one, degree, capacity)
    own_both, weights = together((own_both, (self_one, neigh_one, self_two, neigh_two)))
    slots = exchange(asked)
    inputs = gather((own_both,))
    both_t, both_own, mirror_own, self_two_own, neigh_two_own = turn_weights(feat, me, *weights)
    slots, both_t, both_own, mirror_own, self_two_own, neigh_two_own = together(
        (slots, both_t, both_own, mirror_own, self_two_own, neigh_two_own)
    )
    mirror_mean = call(
        functools.partial(collect_body, order),
        jax.ShapeDtypeStruct((feats, mirrors), BF16),
        (slots, replicas),
        flops=2 * slots.size * mirrors,
        moved=2 * slots.size,
    )
    mirror_mean, kept_masks = together((mirror_mean, kept_masks))
    means = gather((mirror_mean,), last)
    near_masks = call(
        bring_body,
        jax.ShapeDtypeStruct(masks.shape, MASK),
        (kept_masks,),
        hbm=(0,),
        limit=44,
        scratch=(pltpu.SemaphoreType.DMA((PIECES,)),),
        moved=2 * masks.size,
    )
    hidden, self_part = call(
        functools.partial(hidden_body, feat),
        (
            jax.ShapeDtypeStruct((hidden_feats, masters), BF16),
            jax.ShapeDtypeStruct((self_two_own.shape[0], masters), F32),
        ),
        (both_t, both_own, self_two_own) + inputs,
        flops=2 * masters * (4 * self_one.size + self_two_own.size),
        moved=masters * 1024,
    )
    means, near_masks, hidden, self_part, neigh_two_own = together(
        (means, near_masks, hidden, self_part, neigh_two_own)
    )
    own_two, outgoing = second_sums(
        order, cols, gather((mirror_in,)), gather(means), mirror_own, hidden, near_masks, replicas, capacity
    )
    mean_two = call(
        second_mean_body,
        jax.ShapeDtypeStruct((hidden_feats, masters), BF16),
        (exchange(outgoing), rows, own_two, degree),
        flops=2 * hidden_feats * dom * capacity * masters,
        moved=2 * hidden_feats * dom * capacity,
    )
    blocks = gather((mean_two,))
    total = self_part
    for start, stop in ((0, 3), (3, 4)):
        weights = neigh_two_own[:, start * hidden_feats : stop * hidden_feats]
        total = embed(weights, total, blocks[start:stop], BF16 if stop == feat else F32)
    return total


def solution(mesh):
    return jax.shard_map(
        on_device,
        mesh=mesh,
        in_specs=(
            P("feat", "dom"),
            P("dom", None, None, None),
            P("dom", None),
            P(None, "dom"),
            P("dom"),
            P(),
            P(),
            P(),
            P(),
        ),
        out_specs=P("feat", "dom"),
        check_vma=False,
    )
```
